128 devices in a mesh: leaf: 128 (over x, z, y, core).
Axes of the slice: x: 4, y: 4, z: 4, core: 2. Of those that a mesh axis runs over, the one named last changes fastest.
Arguments:
- points: bfloat16 [1048576, 128], P('leaf'), may hold values from -6 to 6
- leaf_basis: bfloat16 [16384, 64, 32], P('leaf'), may hold values from -0.75 to 0.75
- local_transfer: bfloat16 [32640, 32, 32], P('leaf'), may hold values from -0.75 to 0.75
- top_transfer: bfloat16 [128, 32, 32], replicated, may hold values from -0.75 to 0.75
- local_coupling: bfloat16 [32640, 8, 32, 32], P('leaf'), may hold values from -0.375 to 0.375
- local_lists: int32 [32640, 8], P('leaf'), may hold values from -1 to 16383, as said below
- top_coupling: bfloat16 [128, 8, 32, 32], replicated, may hold values from -0.375 to 0.375
- top_lists: int32 [128, 8], replicated, may hold values from -1 to 127, as said below
- near_blocks: bfloat16 [16384, 6, 64, 64], P('leaf'), may hold values from -0.3125 to 0.3125
- near_lists: int32 [16384, 6], P('leaf'), may hold values from -1 to 16383, as said below
Outputs:
- product: bfloat16 [1048576, 128], P('leaf')
The draws below stay inside these ranges and needn't reach their ends.
Inputs may be any that keep to these rules, and one draw needn't show every extreme that they name: `local_lists`: space is cut into 128 slabs one leaf box thick, subtree d being slab d; inside a slab the tree halves the cross-section alternately along its two directions, and a node at depth TD + k is a cell of that level's grid. Partners are children of the node's parent's neighbouring cells (in slabs d - 1, d, d + 1) that are not adjacent to the node; they are distinct within a row, and rows at depths TD to TD + 2 are empty. `top_lists`: rows of nodes at depths 0 and 1 are empty; other partners are distinct nodes of the same depth, two or more positions away from the node. `near_lists`: slot 0 is the leaf itself; the others are distinct leaves whose boxes touch the leaf's box, in the leaf's own slab or the slabs beside it.
All inputs are finite; a program needn't handle non-finite values.
Results may differ from the reference program's by a relative error of at most 0.028.
Values may be sent and summed in bfloat16 or wider, within the bound.
No kernel may reach another device: no remote copies, remote signals or barrier semaphores. Data moves between devices by JAX's collectives and lax.ppermute only.
A program may use at most 192 MiB of HBM per device.

```python
import jax
import jax.numpy as jnp

LEAF = 64
RANK = 32
NV = 128
LEVELS_DEV = 7
ADM = 8
TOP_ADM = 8
NEAR = 6
LEAF_DEV = 128
LEAVES = 16384
POINTS = 1048576
N_LEAF = 128


def depth_of(values, most):
    depth_now = jnp.zeros_like(values)
    for bit_pos in range(1, most + 1):
        depth_now = depth_now + (values >= 2 ** bit_pos).astype(jnp.int32)
    return depth_now


def cell_of(node_pos, depth_now, most):
    cell_y = jnp.zeros_like(node_pos)
    cell_z = jnp.zeros_like(node_pos)
    for step_pos in range(1, most + 1):
        active = step_pos <= depth_now
        shift_by = jnp.maximum(depth_now - step_pos, 0).astype(jnp.int32)
        bit_now = jnp.right_shift(node_pos, shift_by) & 1
        if step_pos % 2 == 1:
            cell_y = jnp.where(active, cell_y * 2 + bit_now, cell_y)
        else:
            cell_z = jnp.where(active, cell_z * 2 + bit_now, cell_z)
    return (cell_y, cell_z)


def node_of(cell_y, cell_z, depth_now, most):
    bits_y = (depth_now + 1) // 2
    bits_z = depth_now // 2
    node_pos = jnp.zeros_like(cell_y)
    for step_pos in range(1, most + 1):
        active = step_pos <= depth_now
        if step_pos % 2 == 1:
            shift_by = jnp.maximum(bits_y - (step_pos + 1) // 2, 0).astype(jnp.int32)
            bit_now = jnp.right_shift(cell_y, shift_by) & 1
        else:
            shift_by = jnp.maximum(bits_z - step_pos // 2, 0).astype(jnp.int32)
            bit_now = jnp.right_shift(cell_z, shift_by) & 1
        node_pos = jnp.where(active, node_pos * 2 + bit_now, node_pos)
    return node_pos


def distinct(chosen, valid):
    columns = []
    for slot_idx in range(chosen.shape[1]):
        keep = valid[:, slot_idx]
        for prior in range(slot_idx):
            keep = keep & ((chosen[:, slot_idx] != chosen[:, prior]) | ~valid[:, prior])
        columns.append(keep)
    keep_all = jnp.stack(columns, axis=1)
    return jnp.where(keep_all, chosen, -1).astype(jnp.int32)


def draw_local_lists(key, part):
    key = jax.random.fold_in(key, 11)
    nodes_dev = 2 * LEAF_DEV - 1
    row_count = N_LEAF * nodes_dev
    row_ids = jnp.arange(row_count, dtype=jnp.int32)
    device_ids = (row_ids // nodes_dev)[:, None]
    heap_pos = row_ids % nodes_dev + 1
    depth_now = depth_of(heap_pos, LEVELS_DEV)[:, None]
    node_pos = heap_pos[:, None] - jnp.left_shift(1, depth_now)
    cell_y, cell_z = cell_of(node_pos, depth_now, LEVELS_DEV)
    parent_depth = jnp.maximum(depth_now - 1, 0)
    par_y, par_z = cell_of(node_pos // 2, parent_depth, LEVELS_DEV)
    par_ny = jnp.left_shift(1, (parent_depth + 1) // 2)
    par_nz = jnp.left_shift(1, parent_depth // 2)
    key_slab, key_y, key_z, key_child = jax.random.split(key, 4)
    shape_now = (row_count, ADM)
    slab_step = jax.random.randint(key_slab, shape_now, -1, 2)
    slot_ids = jnp.arange(ADM, dtype=jnp.int32)[None, :]
    slab_step = jnp.where(slot_ids == 0, jnp.where(device_ids < N_LEAF - 1, 1, -1), slab_step)
    slab_step = jnp.where(slot_ids == 1, jnp.where(device_ids > 0, -1, 1), slab_step)
    other_dev = device_ids + slab_step
    other_py = par_y + jax.random.randint(key_y, shape_now, -1, 2)
    other_pz = par_z + jax.random.randint(key_z, shape_now, -1, 2)
    child_bit = jax.random.randint(key_child, shape_now, 0, 2)
    other_pos = 2 * node_of(jnp.clip(other_py, 0, par_ny - 1), jnp.clip(other_pz, 0, par_nz - 1), parent_depth, LEVELS_DEV) + child_bit
    other_y, other_z = cell_of(other_pos, depth_now, LEVELS_DEV)
    apart = jnp.maximum(jnp.abs(other_y - cell_y), jnp.abs(other_z - cell_z)) >= 2
    valid = (depth_now >= 3) & (other_dev >= 0) & (other_dev < N_LEAF)
    valid = valid & (other_py >= 0) & (other_py < par_ny) & (other_pz >= 0) & (other_pz < par_nz) & apart
    chosen = other_dev * jnp.left_shift(1, depth_now) + other_pos
    return distinct(chosen, valid)


def draw_top_lists(key, part):
    key = jax.random.fold_in(key, 23)
    node_ids = jnp.arange(N_LEAF, dtype=jnp.int32)
    depth_now = depth_of(jnp.maximum(node_ids, 1), 12)
    spread = jnp.left_shift(1, depth_now).astype(jnp.int32)
    half_way = spread + (node_ids - spread + spread // 2) % spread
    raw_pick = jax.random.randint(key, (N_LEAF, TOP_ADM), 0, 1 << 30)
    chosen = spread[:, None] + raw_pick % spread[:, None]
    slot_ids = jnp.arange(TOP_ADM, dtype=jnp.int32)[None, :]
    chosen = jnp.where(slot_ids == 0, half_way[:, None], chosen)
    valid = (jnp.abs(chosen - node_ids[:, None]) >= 2) & (depth_now[:, None] >= 2)
    return distinct(chosen, valid)


def draw_near_lists(key, part):
    key = jax.random.fold_in(key, 37)
    leaf_ids = jnp.arange(LEAVES, dtype=jnp.int32)[:, None]
    device_ids = leaf_ids // LEAF_DEV
    leaf_pos = leaf_ids % LEAF_DEV
    cell_y, cell_z = cell_of(leaf_pos, LEVELS_DEV, LEVELS_DEV)
    grid_y = 2 ** ((LEVELS_DEV + 1) // 2)
    grid_z = 2 ** (LEVELS_DEV // 2)
    key_slab, key_y, key_z = jax.random.split(key, 3)
    shape_now = (LEAVES, NEAR)
    slot_ids = jnp.arange(NEAR, dtype=jnp.int32)[None, :]
    slab_step = jax.random.randint(key_slab, shape_now, -1, 2)
    step_y = jax.random.randint(key_y, shape_now, -1, 2)
    step_z = jax.random.randint(key_z, shape_now, -1, 2)
    slab_step = jnp.where(slot_ids == 1, jnp.where(device_ids > 0, -1, 1), slab_step)
    step_y = jnp.where(slot_ids <= 1, 0, step_y)
    step_z = jnp.where(slot_ids <= 1, 0, step_z)
    slab_step = jnp.where(slot_ids == 0, 0, slab_step)
    other_dev = device_ids + slab_step
    other_y = cell_y + step_y
    other_z = cell_z + step_z
    valid = (other_dev >= 0) & (other_dev < N_LEAF) & (other_y >= 0) & (other_y < grid_y) & (other_z >= 0) & (other_z < grid_z)
    other_pos = node_of(jnp.clip(other_y, 0, grid_y - 1), jnp.clip(other_z, 0, grid_z - 1), LEVELS_DEV, LEVELS_DEV)
    chosen = other_dev * LEAF_DEV + other_pos
    return distinct(chosen, valid)


def block_levels(rng, dims, cuts, least, high):
    def one(position, parts):
        draws = jax.random.uniform(jax.random.fold_in(jax.random.fold_in(rng, 6), position), (parts,), jnp.float32, least / len(cuts), high / len(cuts))
        return jnp.repeat(jnp.exp(draws), dims[position] // parts).reshape((-1,) + (1,) * (len(dims) - position - 1))

    loudness = one(*cuts[0])
    for cut in cuts[1:]:
        loudness = loudness * one(*cut)
    return loudness


def gaussian(rng, dims, width, bound, cuts=(), held_as=jnp.bfloat16):
    factor_of = block_levels(rng, dims, cuts, -0.22, 0.18) if cuts else 1.0
    drawn = jax.random.normal(rng, dims, jnp.float32) * width * factor_of
    return jnp.minimum(jnp.maximum(drawn, -bound), bound).astype(held_as)


def setup_inputs(seed: int = 0) -> dict:
    key_of = jax.random.split(jax.random.key(seed), 11)
    points = gaussian(key_of[0], (POINTS, NV), 1.0, 6.0, ((0, 128),))
    leaf_basis = gaussian(key_of[1], (LEAVES, LEAF, RANK), LEAF ** -0.5, 0.75, ((0, 128),))
    local_transfer = gaussian(key_of[2], (N_LEAF * (2 * LEAF_DEV - 1), RANK, RANK), (2 * RANK) ** -0.5, 0.75, ((0, 128),))
    top_transfer = gaussian(key_of[3], (N_LEAF, RANK, RANK), (2 * RANK) ** -0.5, 0.75)
    local_coupling = gaussian(key_of[4], (N_LEAF * (2 * LEAF_DEV - 1), ADM, RANK, RANK), (ADM * RANK) ** -0.5, 0.375, ((0, 128),))
    local_lists = draw_local_lists(jax.random.fold_in(key_of[10], 71), 0)
    top_coupling = gaussian(key_of[6], (N_LEAF, TOP_ADM, RANK, RANK), (TOP_ADM * RANK) ** -0.5, 0.375)
    top_lists = draw_top_lists(jax.random.fold_in(key_of[10], 71), 0)
    near_blocks = gaussian(key_of[8], (LEAVES, NEAR, LEAF, LEAF), (NEAR * LEAF) ** -0.5, 0.3125, ((0, 128),))
    near_lists = draw_near_lists(jax.random.fold_in(key_of[10], 71), 0)
    return {"points": points, "leaf_basis": leaf_basis, "local_transfer": local_transfer, "top_transfer": top_transfer, "local_coupling": local_coupling, "local_lists": local_lists, "top_coupling": top_coupling, "top_lists": top_lists, "near_blocks": near_blocks, "near_lists": near_lists}


def couple(coeff_level, blocks, partner_ids, first_node):
    is_valid = partner_ids >= 0
    positions = jnp.where(is_valid, partner_ids - first_node, 0).astype(jnp.int32)
    total = jnp.zeros((blocks.shape[0], blocks.shape[2], coeff_level.shape[2]), jnp.float32)
    for slot_idx in range(partner_ids.shape[1]):
        picked = coeff_level[positions[:, slot_idx]].astype(jnp.float32)
        picked = jnp.where(is_valid[:, slot_idx, None, None], picked, jnp.float32(0.0))
        total = total + jnp.einsum('mrs,msv->mrv', blocks[:, slot_idx].astype(jnp.float32), picked)
    return total


def reference(points, leaf_basis, local_transfer, top_transfer, local_coupling, local_lists, top_coupling, top_lists, near_blocks, near_lists):
    top_depth = N_LEAF.bit_length() - 1
    nodes_dev = 2 * LEAF_DEV - 1
    leaf_rows = points.reshape(LEAVES, LEAF, NV)
    shaped_transfer = local_transfer.reshape(N_LEAF, nodes_dev, RANK, RANK)
    shaped_coupling = local_coupling.reshape(N_LEAF, nodes_dev, ADM, RANK, RANK)
    shaped_lists = local_lists.reshape(N_LEAF, nodes_dev, ADM)

    def at_depth(array, depth_now):
        lower = 2 ** depth_now - 1
        return array[:, lower:2 * lower + 1].reshape((-1,) + array.shape[2:])

    coeffs = [None] * (LEVELS_DEV + 1)
    coeffs[LEVELS_DEV] = jnp.einsum('lpr,lpv->lrv', leaf_basis.astype(jnp.float32), leaf_rows.astype(jnp.float32)).astype(jnp.bfloat16)
    for depth_now in range(LEVELS_DEV - 1, -1, -1):
        transfers = at_depth(shaped_transfer, depth_now + 1).astype(jnp.float32)
        up_terms = jnp.einsum('crs,crv->csv', transfers, coeffs[depth_now + 1].astype(jnp.float32))
        coeffs[depth_now] = up_terms.reshape(-1, 2, RANK, NV).sum(axis=1).astype(jnp.bfloat16)
    up_terms = jnp.einsum('crs,crv->csv', at_depth(shaped_transfer, 0).astype(jnp.float32), coeffs[0].astype(jnp.float32))
    top_coeffs = {}
    for depth_now in range(top_depth - 1, 1, -1):
        level_coeff = up_terms.reshape(-1, 2, RANK, NV).sum(axis=1).astype(jnp.bfloat16)
        top_coeffs[depth_now] = level_coeff
        if depth_now > 2:
            transfers = top_transfer[2 ** depth_now:2 ** (depth_now + 1)].astype(jnp.float32)
            up_terms = jnp.einsum('crs,crv->csv', transfers, level_coeff.astype(jnp.float32))
    carried = None
    for depth_now in range(2, top_depth):
        lower = 2 ** depth_now
        far_now = couple(top_coeffs[depth_now], top_coupling[lower:2 * lower], top_lists[lower:2 * lower], lower)
        if carried is None:
            carried = far_now
        else:
            parents = jnp.repeat(carried.astype(jnp.bfloat16), 2, axis=0).astype(jnp.float32)
            carried = far_now + jnp.einsum('crs,csv->crv', top_transfer[lower:2 * lower].astype(jnp.float32), parents)
    for depth_now in range(0, LEVELS_DEV + 1):
        far_now = couple(coeffs[depth_now], at_depth(shaped_coupling, depth_now), at_depth(shaped_lists, depth_now), 0)
        parents = jnp.repeat(carried.astype(jnp.bfloat16), 2, axis=0).astype(jnp.float32)
        carried = far_now + jnp.einsum('crs,csv->crv', at_depth(shaped_transfer, depth_now).astype(jnp.float32), parents)
    far_rows = jnp.einsum('lpr,lrv->lpv', leaf_basis.astype(jnp.float32), carried.astype(jnp.bfloat16).astype(jnp.float32))
    near_rows = couple(leaf_rows, near_blocks, near_lists, 0)
    return (far_rows + near_rows).astype(jnp.bfloat16).reshape(POINTS, NV)
```

```python
import jax
import jax.numpy as jnp
import numpy as np
from jax import lax
from jax.experimental import pallas as pl
from jax.experimental.pallas import tpu as pltpu
from jax.sharding import PartitionSpec as P

BF = jnp.bfloat16
F32 = jnp.float32
NT = (((1,), (1,)), ((), ()))
NN = (((1,), (0,)), ((), ()))
TN = (((0,), (0,)), ((), ()))


def dot(a, b, dims=NN):
    return lax.dot_general(a, b, dims, preferred_element_type=F32)


def eye(rows, cols):
    return (lax.broadcasted_iota(jnp.int32, (rows, cols), 0)
            == lax.broadcasted_iota(jnp.int32, (rows, cols), 1)).astype(BF)


def steps(count, width, body):
    def trip(t, carry):
        for u in range(width):
            body(t * width + u)
        return carry
    lax.fori_loop(0, count // width, trip, 0)


def near_prep_kernel(blocks, out, wide):
    slots, rows, cols, leaves = blocks.shape
    ident = eye(leaves, leaves)
    chunks = slots * cols // 128

    def turn(r):
        both = blocks[:, r].reshape(slots * cols, leaves)
        turned = dot(ident, both, NT)
        for j in range(chunks):
            wide[j, pl.ds(pl.multiple_of(r * leaves, leaves), leaves), :] = turned[:, j * 128:(j + 1) * 128]

    steps(rows, 4, turn)

    def pick(leaf):
        parts = [wide[j, pl.ds(leaf, rows, stride=leaves), :].astype(BF) for j in range(chunks)]
        for j in range(chunks):
            out[leaf, :, j * 128:(j + 1) * 128] = parts[j]

    steps(leaves, 8, pick)


def near_prep(blocks_t, part=16):
    slots, rows, cols, leaves = blocks_t.shape
    width = slots * cols
    return pl.pallas_call(
        near_prep_kernel,
        grid=(rows // part,),
        in_specs=[pl.BlockSpec((slots, part, cols, leaves), lambda i: (0, i, 0, 0))],
        out_specs=pl.BlockSpec((leaves, part, width), lambda i: (0, i, 0)),
        out_shape=jax.ShapeDtypeStruct((leaves, rows, width), BF),
        scratch_shapes=[pltpu.VMEM((width // 128, part * leaves, 128), F32)],
        compiler_params=pltpu.CompilerParams(vmem_limit_bytes=40 << 20),
        name="near_prep",
    )(blocks_t)


def coup_prep_kernel(blocks, out, wide):
    slots, rows, cols, nodes = blocks.shape
    padded = out.shape[0]
    ident = eye(padded, nodes)
    chunks = slots * cols // 128

    def turn(r):
        both = blocks[:, r].reshape(slots * cols, nodes)
        turned = dot(ident, both, NT)
        for j in range(chunks):
            wide[j, pl.ds(pl.multiple_of(r * padded, padded), padded), :] = turned[:, j * 128:(j + 1) * 128]

    steps(rows, 4, turn)

    def pick(node):
        for j in range(chunks):
            out[node, :, j * 128:(j + 1) * 128] = wide[j, pl.ds(node, rows, stride=padded), :].astype(BF)

    steps(padded, 8, pick)


def coup_prep(blocks_t, part=16):
    slots, rows, cols, nodes = blocks_t.shape
    width = slots * cols
    padded = (nodes + 7) // 8 * 8
    return pl.pallas_call(
        coup_prep_kernel,
        grid=(rows // part,),
        in_specs=[pl.BlockSpec((slots, part, cols, nodes), lambda i: (0, i, 0, 0))],
        out_specs=pl.BlockSpec((padded, part, width), lambda i: (0, i, 0)),
        out_shape=jax.ShapeDtypeStruct((padded, rows, width), BF),
        scratch_shapes=[pltpu.VMEM((width // 128, part * padded, 128), F32)],
        compiler_params=pltpu.CompilerParams(vmem_limit_bytes=40 << 20),
        name="coup_prep",
    )(blocks_t)


def upward_kernel(points, basis, transfer, coeff, root, basis_out, transfer_out, wide_b, wide_e):
    size, rank, leaves = basis.shape
    nodes = transfer.shape[2]
    padded = nodes + 1
    ident = eye(leaves, leaves)
    ident_e = eye(padded, nodes)

    def turn_b(p):
        wide_b[pl.ds(pl.multiple_of(p * leaves, leaves), leaves), 0:rank] = dot(ident, basis[p], NT)

    steps(size, 8, turn_b)

    def turn_e(r):
        wide_e[pl.ds(pl.multiple_of(r * padded, padded), padded), 0:rank] = dot(ident_e, transfer[r], NT)

    steps(rank, 4, turn_e)

    def leaf_step(leaf):
        mine = wide_b[pl.ds(leaf, size, stride=leaves), :].astype(BF)[:, 0:rank]
        basis_out[leaf] = mine
        x = points[pl.ds(pl.multiple_of(leaf * size, size), size), :]
        at = pl.multiple_of((leaves - 1 + leaf) * rank, rank)
        coeff[pl.ds(at, rank), :] = dot(mine, x, TN).astype(BF)

    steps(leaves, 8, leaf_step)

    def e_of(node):
        mine = wide_e[pl.ds(node, rank, stride=padded), :].astype(BF)[:, 0:rank]
        transfer_out[node] = mine
        return mine

    count = leaves // 2
    while count >= 1:
        def node_step(p, count=count):
            left = 2 * count - 1 + 2 * p
            both = jnp.concatenate([e_of(left), e_of(left + 1)], axis=0)
            kids = coeff[pl.ds(pl.multiple_of(left * rank, rank), 2 * rank), :]
            at = pl.multiple_of((count - 1 + p) * rank, rank)
            coeff[pl.ds(at, rank), :] = dot(both, kids, TN).astype(BF)
        steps(count, min(count, 8), node_step)
        count //= 2
    root[...] = dot(e_of(0), coeff[0:rank, :], TN)
    coeff[pl.ds(nodes * rank, rank), :] = jnp.zeros((rank, coeff.shape[1]), BF)


def upward(points, basis_t, transfer_t):
    size, rank, leaves = basis_t.shape
    padded = transfer_t.shape[2] + 1
    vecs = points.shape[1]
    return pl.pallas_call(
        upward_kernel,
        out_shape=(
            jax.ShapeDtypeStruct((padded * rank, vecs), BF),
            jax.ShapeDtypeStruct((rank, vecs), F32),
            jax.ShapeDtypeStruct((leaves, size, rank), BF),
            jax.ShapeDtypeStruct((padded, rank, rank), BF),
        ),
        scratch_shapes=[pltpu.VMEM((size * leaves, 128), F32), pltpu.VMEM((rank * padded, 128), F32)],
        compiler_params=pltpu.CompilerParams(vmem_limit_bytes=48 << 20),
        name="upward",
    )(points, basis_t, transfer_t)


def near_kernel(pos, lhs, own, mate, other, out, window, sems):
    i = pl.program_id(0)
    part, size, width = lhs.shape
    slots = width // size
    rows = own.shape[0]

    @pl.when(i == 0)
    def _():
        copies = [pltpu.make_async_copy(src, window.at[pl.ds(n * rows, rows)], sems.at[n])
                  for n, src in enumerate((own, mate, other))]
        for c in copies:
            c.start()
        window[3 * rows:3 * rows + size, :] = jnp.zeros((size, window.shape[1]), BF)
        for c in copies:
            c.wait()

    def leaf_step(l):
        leaf = i * part + l
        rhs = jnp.concatenate(
            [window[pl.ds(pl.multiple_of(pos[s, leaf] * size, size), size), :] for s in range(slots)], axis=0)
        out[pl.ds(pl.multiple_of(l * size, size), size), :] = dot(lhs[l], rhs)

    steps(part, 8, leaf_step)


def near(pos, lhs, own, mate, other, part=32):
    leaves, size, width = lhs.shape
    rows, vecs = own.shape
    any_ = pl.BlockSpec(memory_space=pl.ANY)
    return pl.pallas_call(
        near_kernel,
        grid_spec=pltpu.PrefetchScalarGridSpec(
            num_scalar_prefetch=1,
            grid=(leaves // part,),
            in_specs=[pl.BlockSpec((part, size, width), lambda i, p: (i, 0, 0)), any_, any_, any_],
            out_specs=pl.BlockSpec((part * size, vecs), lambda i, p: (i, 0)),
            scratch_shapes=[pltpu.VMEM((3 * rows + size, vecs), BF), pltpu.SemaphoreType.DMA((3,))],
        ),
        out_shape=jax.ShapeDtypeStruct((rows, vecs), F32),
        compiler_params=pltpu.CompilerParams(vmem_limit_bytes=40 << 20),
        name="near",
    )(pos, lhs, own, mate, other)


def final_kernel(pos, lhs, own, mate, other, transfer, basis, above, near_rows, out, window, far, down, sems):
    rank = transfer.shape[1]
    leaves, size, _ = basis.shape
    slots = lhs.shape[2] // rank
    first = 7
    rows = (2 * leaves - 1 - first) * rank
    copies = [pltpu.make_async_copy(src.at[pl.ds(first * rank, rows)], window.at[pl.ds(n * rows, rows)], sems.at[n])
              for n, src in enumerate((own, mate, other))]
    for c in copies:
        c.start()
    window[3 * rows:3 * rows + rank, :] = jnp.zeros((rank, window.shape[1]), BF)
    for c in copies:
        c.wait()

    def couple(n):
        node = n + first
        rhs = jnp.concatenate(
            [window[pl.ds(pl.multiple_of(pos[s, node] * rank, rank), rank), :] for s in range(slots)], axis=0)
        far[pl.ds(pl.multiple_of(n * rank, rank), rank), :] = dot(lhs[node], rhs)

    steps(2 * leaves - 1 - first, 8, couple)

    down[0:rank, :] = dot(transfer[0], above[...].astype(BF)).astype(BF)
    count = 2
    while count < leaves:
        def node_step(p, count=count):
            node = count - 1 + p
            parent = (node - 1) // 2 if isinstance(node, int) else lax.shift_right_logical(node - 1, 1)
            got = dot(transfer[node], down[pl.ds(pl.multiple_of(parent * rank, rank), rank), :])
            if count >= 8:
                got = got + far[pl.ds(pl.multiple_of((node - first) * rank, rank), rank), :]
            down[pl.ds(pl.multiple_of(node * rank, rank), rank), :] = got.astype(BF)
        steps(count, min(count, 8), node_step)
        count *= 2

    def leaf_step(leaf):
        node = leaves - 1 + leaf
        parent = lax.shift_right_logical(node - 1, 1)
        got = dot(transfer[node], down[pl.ds(pl.multiple_of(parent * rank, rank), rank), :])
        got = got + far[pl.ds(pl.multiple_of((node - first) * rank, rank), rank), :]
        at = pl.ds(pl.multiple_of(leaf * size, size), size)
        out[at, :] = (dot(basis[leaf], got.astype(BF)) + near_rows[at, :]).astype(BF)

    steps(leaves, 8, leaf_step)


def final(pos, lhs, own, mate, other, transfer, basis, above, near_rows):
    leaves, size, rank = basis.shape
    vecs = own.shape[1]
    any_ = pl.BlockSpec(memory_space=pl.ANY)
    vm = pl.BlockSpec(memory_space=pltpu.VMEM)
    rows = (2 * leaves - 8) * rank
    return pl.pallas_call(
        final_kernel,
        in_specs=[pl.BlockSpec(memory_space=pltpu.SMEM), vm, any_, any_, any_, vm, vm, vm, vm],
        out_shape=jax.ShapeDtypeStruct((leaves * size, vecs), BF),
        scratch_shapes=[
            pltpu.VMEM((3 * rows + rank, vecs), BF),
            pltpu.VMEM((rows, vecs), F32),
            pltpu.VMEM(((leaves - 1) * rank, vecs), BF),
            pltpu.SemaphoreType.DMA((3,)),
        ],
        compiler_params=pltpu.CompilerParams(vmem_limit_bytes=56 << 20),
        name="final",
    )(pos, lhs, own, mate, other, transfer, basis, above, near_rows)


def top_kernel(where_am_i, lists, gathered, transfer, coupling, out, wide_e, wide_c, coeff):
    rank, _, nodes = transfer.shape
    slots = coupling.shape[0]
    chips = nodes // 2
    me = where_am_i[0]
    depths = nodes.bit_length() - 1
    ident = eye(nodes, nodes)
    row = lax.broadcasted_iota(jnp.int32, (8, nodes), 0)
    lane = lax.broadcasted_iota(jnp.int32, (8, nodes), 1)
    ancestor = lax.shift_right_logical(nodes + me, jnp.maximum(depths - 2 - row, 0))
    picks = ((lane == ancestor) & (row < depths - 2)).astype(BF)

    def turn(r):
        wide_e[pl.ds(pl.multiple_of(r * nodes, nodes), nodes), 0:rank] = dot(ident, transfer[r], NT)
        both = coupling[:, r].reshape(slots * rank, nodes)
        turned = dot(picks, both, NT)
        for j in range(2):
            wide_c[j, pl.ds(pl.multiple_of(r * 8, 8), 8), :] = turned[:, j * 128:(j + 1) * 128]

    steps(rank, 4, turn)
    coeff[0:rank, :] = jnp.zeros((rank, coeff.shape[1]), BF)

    def place(q):
        seen = q ^ lax.shift_right_logical(me, 1)
        coeff[pl.ds(pl.multiple_of((chips + q) * rank, rank), rank), :] = (
            gathered[pl.ds(pl.multiple_of(seen * rank, rank), rank), :])

    steps(chips, 8, place)

    def e_of(node):
        return wide_e[pl.ds(node, rank, stride=nodes), :].astype(BF)[:, 0:rank]

    count = chips // 2
    while count >= 4:
        def node_step(p, count=count):
            node = count + p
            both = jnp.concatenate([e_of(2 * node), e_of(2 * node + 1)], axis=0)
            kids = coeff[pl.ds(pl.multiple_of(2 * node * rank, rank), 2 * rank), :]
            coeff[pl.ds(pl.multiple_of(node * rank, rank), rank), :] = dot(both, kids, TN).astype(BF)
        steps(count, min(count, 8), node_step)
        count //= 2

    down = None
    for depth in range(2, depths):
        node = lax.shift_right_logical(nodes + me, depths - depth)
        rhs = jnp.concatenate([
            coeff[pl.ds(pl.multiple_of(jnp.maximum(lists[s, node], 0) * rank, rank), rank), :]
            for s in range(slots)], axis=0)
        lhs = jnp.concatenate(
            [wide_c[j, pl.ds(depth - 2, rank, stride=8), :].astype(BF) for j in range(2)], axis=1)
        far = dot(lhs, rhs)
        down = far if down is None else far + dot(e_of(node), down.astype(BF))
    out[...] = down


def top(me, lists_t, gathered, transfer_t, coupling_t):
    rank, _, nodes = transfer_t.shape
    vecs = gathered.shape[1]
    sm = pl.BlockSpec(memory_space=pltpu.SMEM)
    vm = pl.BlockSpec(memory_space=pltpu.VMEM)
    return pl.pallas_call(
        top_kernel,
        in_specs=[sm, sm, vm, vm, vm],
        out_shape=jax.ShapeDtypeStruct((rank, vecs), F32),
        scratch_shapes=[pltpu.VMEM((rank * nodes, 128), F32), pltpu.VMEM((2, rank * 8, 128), F32),
                        pltpu.VMEM((nodes * rank, vecs), BF)],
        compiler_params=pltpu.CompilerParams(vmem_limit_bytes=32 << 20),
        name="top",
    )(me, lists_t, gathered, transfer_t, coupling_t)


def slots_of(ids, size_log, own, base, per_slab):
    slab = lax.shift_right_arithmetic(ids, size_log)
    inside = ids & (lax.shift_left(jnp.ones_like(size_log), size_log) - 1)
    block = jnp.where(slab == own, 0, jnp.where(slab == (own ^ 1), 1, 2))
    return jnp.where(ids >= 0, block * per_slab + base + inside, 3 * per_slab)


def shards(points, leaf_basis, local_transfer, top_transfer, local_coupling, local_lists,
           top_coupling, top_lists, near_blocks, near_lists):
    leaf_dev, leaf_size, rank = leaf_basis.shape
    nodes = local_transfer.shape[0]
    count = lax.axis_size("leaf")
    own = lax.axis_index("leaf")
    mates = [(i, i ^ 1) for i in range(count)]
    others = [(i, i + 1) for i in range(1, count - 1, 2)]
    others = others + [(j, i) for i, j in others]

    basis_t = jnp.transpose(leaf_basis, (1, 2, 0))
    transfer_t = jnp.transpose(local_transfer, (1, 2, 0))
    points_other = lax.ppermute(points, "leaf", others)
    points_mate = lax.ppermute(points, "leaf", mates)
    coeff, root, basis_rows, transfer_rows = upward(points, basis_t, transfer_t)
    coeff_other = lax.ppermute(coeff, "leaf", others)
    coeff_mate = lax.ppermute(coeff, "leaf", mates)
    gathered = (root + lax.ppermute(root, "leaf", mates)).astype(BF)
    step = 2
    while step < count:
        came = lax.ppermute(gathered, "leaf", [(i, i ^ step) for i in range(count)])
        gathered = jnp.concatenate([gathered, came], axis=0)
        step *= 2
    lhs_near = near_prep(jnp.transpose(near_blocks, (1, 2, 3, 0)))
    lhs_coup = coup_prep(jnp.transpose(local_coupling, (1, 2, 3, 0)))
    above = top(own[None], top_lists.T, gathered, jnp.transpose(top_transfer, (1, 2, 0)),
                jnp.transpose(top_coupling, (1, 2, 3, 0)))
    leaf_log = leaf_dev.bit_length() - 1
    near_pos = slots_of(near_lists.T, jnp.full((1, leaf_dev), leaf_log, jnp.int32), own, 0, leaf_dev)
    near_rows = near(near_pos, lhs_near, points, points_mate, points_other)
    level = np.array([[(n + 1).bit_length() - 1 for n in range(nodes)]], np.int32)
    coup_pos = slots_of(local_lists.T, jnp.asarray(level), own, jnp.asarray(2 ** level - 8), nodes - 7)
    return final(coup_pos, lhs_coup, coeff, coeff_mate, coeff_other, transfer_rows, basis_rows, above, near_rows)


def solution(mesh):
    leaf, whole = P("leaf"), P()
    return jax.shard_map(
        shards,
        mesh=mesh,
        in_specs=(leaf, leaf, leaf, whole, leaf, leaf, whole, whole, leaf, leaf),
        out_specs=leaf,
        check_vma=False,
    )
```

```python
import jax
import jax.numpy as jnp
import numpy as np
from jax import lax
from jax.experimental import pallas as pl
from jax.experimental.pallas import tpu as pltpu
from jax.sharding import PartitionSpec as P

BF = jnp.bfloat16
F32 = jnp.float32
NT = (((1,), (1,)), ((), ()))
NN = (((1,), (0,)), ((), ()))
TN = (((0,), (0,)), ((), ()))
PAD = 8
FIRST = 7
SCALE = 40000
VMEM = 28 << 20
ANY = pl.BlockSpec(memory_space=pl.ANY)


def dot(a, b, dims=NN):
    return lax.dot_general(a, b, dims, preferred_element_type=F32)


def cost(us):
    return pl.CostEstimate(flops=0, bytes_accessed=us * SCALE, transcendentals=0)


def eye(rows, cols):
    return (lax.broadcasted_iota(jnp.int32, (rows, cols), 0)
            == lax.broadcasted_iota(jnp.int32, (rows, cols), 1)).astype(BF)


def batch(count, width, load, work, store):
    width = min(width, count)

    def trip(t, carry):
        at = [t * width + u for u in range(width)]
        got = [load(i) for i in at]
        done = [work(*g) for g in got]
        for i, d in zip(at, done):
            store(i, d)
        return carry

    if count == width:
        trip(0, 0)
    else:
        lax.fori_loop(0, count // width, trip, 0)


def rows_at(index, height, many=1):
    start = index * height
    return pl.ds(start if isinstance(start, int) else pl.multiple_of(start, height), many * height)


def put(wide, at, value):
    width = value.shape[1]
    for j in range(wide.shape[0]):
        piece = value[:, j * 128:min(width, (j + 1) * 128)]
        wide[j, pl.ds(at if isinstance(at, int) else pl.multiple_of(at, 8), value.shape[0]), 0:piece.shape[1]] = piece


def turn_kernel(blocks, extra, out, wide):
    slots, rows, cols, lanes = blocks.shape
    count, _, width = out.shape
    ident = eye(count, lanes)
    step = count + PAD
    chunks = wide.shape[0]

    batch(rows, 8,
          lambda r: (jnp.concatenate([blocks[:, r].reshape(slots * cols, lanes), extra[r]], axis=0),),
          lambda both: dot(ident, both, NT),
          lambda r, turned: put(wide, r * step, turned))

    def store(i, parts):
        for j in range(chunks):
            end = min(width, (j + 1) * 128)
            out[i, :, j * 128:end] = parts[j][:, 0:end - j * 128]

    batch(count, 16,
          lambda i: [wide[j, pl.ds(i, rows, stride=step), :] for j in range(chunks)],
          lambda *parts: [p.astype(BF) for p in parts], store)


def turn(blocks_t, extra_t, name, first, rows, part=16):
    slots, _, cols, lanes = blocks_t.shape
    skip = first // part
    width = slots * cols + extra_t.shape[1]
    count = (lanes + 7) // 8 * 8
    chunks = (width + 127) // 128
    return pl.pallas_call(
        turn_kernel,
        grid=(rows // part,),
        in_specs=[pl.BlockSpec((slots, part, cols, lanes), lambda i: (0, i + skip, 0, 0)),
                  pl.BlockSpec((part,) + extra_t.shape[1:], lambda i: (i + skip, 0, 0))],
        out_specs=pl.BlockSpec((count, part, width), lambda i: (0, i, 0)),
        out_shape=jax.ShapeDtypeStruct((count, rows, width), BF),
        scratch_shapes=[pltpu.VMEM((chunks, part * (count + PAD), 128), F32)],
        compiler_params=pltpu.CompilerParams(vmem_limit_bytes=VMEM),
        cost_estimate=cost(max(1, rows * count // 1024)),
        name=name,
    )(blocks_t, extra_t)


def upward_kernel(me, points_in, basis_in, transfer_in, coeff, keep, give, points, basis, transfer, wide_b, wide_e, sems):
    size, rank, leaves = basis.shape
    copies = [pltpu.make_async_copy(src, dst, sems.at[n])
              for n, (src, dst) in enumerate(((basis_in, basis), (transfer_in, transfer), (points_in, points)))]
    for c in copies:
        c.start()
    nodes = transfer.shape[2]
    padded = nodes + 1
    ident = eye(leaves, leaves)
    ident_e = eye(padded, nodes)
    step_b, step_e = leaves + PAD, padded + PAD

    copies[0].wait()
    batch(size, 16, lambda p: (basis[p],), lambda b: dot(ident, b, NT), lambda p, v: put(wide_b, p * step_b, v))
    copies[1].wait()
    batch(rank, 16, lambda r: (transfer[r],), lambda b: dot(ident_e, b, NT), lambda r, v: put(wide_e, r * step_e, v))

    copies[2].wait()

    def store_leaf(leaf, got):
        coeff[rows_at(leaves - 1 + leaf, rank), :] = got

    batch(leaves, 32,
          lambda leaf: (wide_b[0, pl.ds(leaf, size, stride=step_b), :], points[rows_at(leaf, size), :]),
          lambda mine, x: dot(mine.astype(BF)[:, 0:rank], x, TN).astype(BF), store_leaf)

    def e_of(node):
        return wide_e[0, pl.ds(node, rank, stride=step_e), :]

    def pair_work(left, right, kids):
        both = jnp.concatenate([left, right], axis=0).astype(BF)[:, 0:rank]
        return dot(both, kids, TN).astype(BF)

    count = leaves // 2
    while count >= 1:
        def load(p, count=count):
            left = 2 * count - 1 + 2 * p
            return e_of(left), e_of(left + 1), coeff[rows_at(left, rank, 2), :]

        def store(p, got, count=count):
            coeff[rows_at(count - 1 + p, rank), :] = got

        batch(count, 32, load, pair_work, store)
        count //= 2
    root = dot(e_of(0).astype(BF)[:, 0:rank], coeff[0:rank, :], TN)
    low, high = root[0:rank // 2], root[rank // 2:]
    odd = (me[0] & 1) == 1
    keep[...] = jnp.where(odd, high, low)
    give[...] = jnp.where(odd, low, high)
    coeff[pl.ds(nodes * rank, rank), :] = jnp.zeros((rank, coeff.shape[1]), BF)


def upward(me, points, basis_t, transfer_t):
    size, rank, leaves = basis_t.shape
    padded = transfer_t.shape[2] + 1
    vecs = points.shape[1]
    return pl.pallas_call(
        upward_kernel,
        in_specs=[pl.BlockSpec(memory_space=pltpu.SMEM)] + [pl.BlockSpec(memory_space=pltpu.HBM)] * 3,
        out_shape=(jax.ShapeDtypeStruct((padded * rank, vecs), BF),)
        + (jax.ShapeDtypeStruct((rank // 2, vecs), F32),) * 2,
        scratch_shapes=[pltpu.VMEM(points.shape, BF), pltpu.VMEM(basis_t.shape, BF), pltpu.VMEM(transfer_t.shape, BF),
                        pltpu.VMEM((1, size * (leaves + PAD), 128), F32),
                        pltpu.VMEM((1, rank * (padded + PAD), 128), F32), pltpu.SemaphoreType.DMA((3,))],
        compiler_params=pltpu.CompilerParams(vmem_limit_bytes=VMEM),
        cost_estimate=cost(7),
        name="upward",
    )(me, points, basis_t, transfer_t)


def top_kernel(where_am_i, lists, mine_in, mate_in, transfer_in, coupling_in, out, mine, mate, transfer, coupling,
               wide_e, wide_c, coeff, sems):
    rank, _, nodes = transfer.shape
    copies = [pltpu.make_async_copy(src, dst, sems.at[n]) for n, (src, dst) in enumerate(
        ((transfer_in, transfer), (mine_in, mine), (mate_in, mate), (coupling_in, coupling)))]
    for c in copies:
        c.start()
    slots = coupling.shape[0]
    chips = nodes // 2
    me = where_am_i[0]
    depths = nodes.bit_length() - 1
    step = nodes + PAD
    ident = eye(nodes, nodes)
    row = lax.broadcasted_iota(jnp.int32, (8, nodes), 0)
    lane = lax.broadcasted_iota(jnp.int32, (8, nodes), 1)
    ancestor = lax.shift_right_logical(nodes + me, jnp.maximum(depths - 2 - row, 0))
    picks = ((lane == ancestor) & (row < depths - 2)).astype(BF)

    copies[0].wait()
    batch(rank, 16, lambda r: (transfer[r],), lambda e: dot(ident, e, NT), lambda r, v: put(wide_e, r * step, v))
    coeff[0:rank, :] = jnp.zeros((rank, coeff.shape[1]), BF)

    chip = lax.shift_right_logical(me, 1)
    half = rank // 2
    copies[1].wait()
    copies[2].wait()
    for held, core in ((mine, me & 1), (mate, 1 - (me & 1))):
        def place(q, got, core=core):
            seen = chip ^ q ^ (lax.shift_right_logical(q, 1) & 0b010101)
            coeff[pl.ds(pl.multiple_of((chips + seen) * rank + core * half, half), half), :] = got

        batch(chips, 16, lambda q, held=held: (held[rows_at(q, half), :],), lambda v: v, place)

    def e_of(node):
        return wide_e[0, pl.ds(node, rank, stride=step), :]

    def pair_work(left, right, kids):
        both = jnp.concatenate([left, right], axis=0).astype(BF)[:, 0:rank]
        return dot(both, kids, TN).astype(BF)

    count = chips // 2
    while count >= 4:
        def load(p, count=count):
            left = 2 * (count + p)
            return e_of(left), e_of(left + 1), coeff[rows_at(left, rank, 2), :]

        def store(p, got, count=count):
            coeff[rows_at(count + p, rank), :] = got

        batch(count, 32, load, pair_work, store)
        count //= 2

    copies[3].wait()
    batch(rank, 16, lambda r: (coupling[:, r].reshape(slots * rank, nodes),), lambda c: dot(picks, c, NT),
          lambda r, v: put(wide_c, r * 8, v))
    fars = []
    for depth in range(2, depths):
        node = lax.shift_right_logical(nodes + me, depths - depth)
        rhs = jnp.concatenate([coeff[rows_at(jnp.maximum(lists[s, node], 0), rank), :] for s in range(slots)], axis=0)
        lhs = jnp.concatenate(
            [wide_c[j, pl.ds(depth - 2, rank, stride=8), :].astype(BF) for j in range(wide_c.shape[0])], axis=1)
        fars.append((node, dot(lhs, rhs)))
    down = None
    for node, far in fars:
        down = far if down is None else far + dot(e_of(node).astype(BF)[:, 0:rank], down.astype(BF))
    out[...] = down.astype(BF)


def top(me, lists_t, mine, mate, transfer_t, coupling_t):
    rank, _, nodes = transfer_t.shape
    vecs = mine.shape[1]
    chunks = coupling_t.shape[0] * rank // 128
    sm = pl.BlockSpec(memory_space=pltpu.SMEM)
    hbm = pl.BlockSpec(memory_space=pltpu.HBM)
    return pl.pallas_call(
        top_kernel,
        in_specs=[sm, sm, ANY, ANY, hbm, hbm],
        out_shape=jax.ShapeDtypeStruct((rank, vecs), BF),
        scratch_shapes=[pltpu.VMEM(mine.shape, BF), pltpu.VMEM(mine.shape, BF), pltpu.VMEM(transfer_t.shape, BF), pltpu.VMEM(coupling_t.shape, BF),
                        pltpu.VMEM((1, rank * (nodes + PAD), 128), F32), pltpu.VMEM((chunks, rank * 8, 128), F32),
                        pltpu.VMEM((nodes * rank, vecs), BF), pltpu.SemaphoreType.DMA((4,))],
        compiler_params=pltpu.CompilerParams(vmem_limit_bytes=VMEM),
        cost_estimate=cost(4),
        name="top",
    )(me, lists_t, mine, mate, transfer_t, coupling_t)


def down_kernel(parts, pos, own, mate, other, above, *refs):
    lhs_in, (out, *lhs), (window, down, sems) = refs[:parts], refs[parts:2 * parts + 1], refs[2 * parts + 1:]
    nodes, _, width = lhs[0].shape
    rank = above.shape[0]

    def lhs_of(node):
        return jnp.concatenate([a[node] for a in lhs], axis=0)

    nodes = nodes - 1
    leaves = (nodes + 1) // 2
    slots = width // rank - 1
    rows = (nodes - FIRST) * rank
    half = nodes // 2
    lhs_copies = [[pltpu.make_async_copy(src.at[pl.ds(at, size)], dst.at[pl.ds(at, size)], sems.at[3 + 2 * n + k])
                   for n, (src, dst) in enumerate(zip(lhs_in, lhs))]
                  for k, (at, size) in enumerate(((0, half), (half, nodes + 1 - half)))]
    copies = [pltpu.make_async_copy(src.at[pl.ds(FIRST * rank, rows)], window.at[pl.ds(n * rows, rows)], sems.at[n])
              for n, src in enumerate((own, mate, other))]
    for c in lhs_copies[0] + copies + lhs_copies[1]:
        c.start()
    window[3 * rows:3 * rows + rank, :] = jnp.zeros((rank, window.shape[1]), BF)
    for c in lhs_copies[0]:
        c.wait()

    def parent_of(node):
        if isinstance(node, int):
            return down[rows_at((node - 1) // 2, rank), :] if node else above[...]
        return down[rows_at(lax.shift_right_logical(node - 1, 1), rank), :]

    for node in range(FIRST):
        down[rows_at(node, rank), :] = dot(lhs_of(node)[:, slots * rank:], parent_of(node)).astype(BF)
    for c in copies:
        c.wait()

    count = FIRST + 1
    while count <= leaves:
        def load(p, count=count):
            node = count - 1 + p
            return lhs_of(node), jnp.concatenate(
                [window[rows_at(pos[s, node], rank), :] for s in range(slots)] + [parent_of(node)], axis=0)

        def store(p, got, count=count):
            if count == leaves:
                out[rows_at(p, rank), :] = got
            else:
                down[rows_at(count - 1 + p, rank), :] = got

        if count == leaves:
            for c in lhs_copies[1]:
                c.wait()
        batch(count, DB, load, lambda a, b: dot(a, b).astype(BF), store)
        count *= 2


DB = 32


def downward(pos, lhs, own, mate, other, above):
    nodes = lhs[0].shape[0]
    rank = above.shape[0]
    leaves = nodes // 2
    vecs = own.shape[1]
    any_ = pl.BlockSpec(memory_space=pltpu.HBM)
    vm = pl.BlockSpec(memory_space=pltpu.VMEM)
    rows = (nodes - 1 - FIRST) * rank
    return pl.pallas_call(
        lambda *refs: down_kernel(len(lhs), *refs),
        in_specs=[pl.BlockSpec(memory_space=pltpu.SMEM), any_, any_, any_, vm] + [any_] * len(lhs),
        out_shape=jax.ShapeDtypeStruct((leaves * rank, vecs), BF),
        scratch_shapes=[pltpu.VMEM(a.shape, BF) for a in lhs]
        + [pltpu.VMEM((3 * rows + rank, vecs), BF), pltpu.VMEM((leaves * rank, vecs), BF),
           pltpu.SemaphoreType.DMA((3 + 2 * len(lhs),))],
        compiler_params=pltpu.CompilerParams(vmem_limit_bytes=VMEM),
        cost_estimate=cost(9),
        name="downward",
    )(pos, own, mate, other, above, *lhs)


def rows_kernel(parts, count, pos, down, *refs):
    lhs, pieces, (out, window, sems) = refs[:parts], refs[parts:parts + count], refs[parts + count:]
    i = pl.program_id(0)
    part, _, width = lhs[0].shape
    size = sum(a.shape[1] for a in lhs)
    rank = down.shape[0] // part
    slots = (width - rank) // size

    @pl.when(i == 0)
    def _():
        copies, at = [], 0
        for n, src in enumerate(pieces):
            copies.append(pltpu.make_async_copy(src, window.at[pl.ds(at, src.shape[0])], sems.at[n]))
            at += src.shape[0]
        for c in copies:
            c.start()
        window[at:at + size, :] = jnp.zeros((size, window.shape[1]), BF)
        for c in copies:
            c.wait()

    def load(l):
        return jnp.concatenate([a[l] for a in lhs], axis=0), jnp.concatenate(
            [window[rows_at(pos[s, i * part + l], size), :] for s in range(slots)] + [down[rows_at(l, rank), :]], axis=0)

    def store(l, got):
        out[rows_at(l, size), :] = got

    batch(part, 16, load, lambda a, b: dot(a, b).astype(BF), store)


def leaf_rows(pos, lhs, down, *pieces):
    leaves, _, width = lhs[0].shape
    size = sum(a.shape[1] for a in lhs)
    rows, vecs = pieces[0].shape
    rank = down.shape[0] // leaves
    part = 32
    any_ = pl.BlockSpec(memory_space=pltpu.HBM)
    return pl.pallas_call(
        lambda *refs: rows_kernel(len(lhs), len(pieces), *refs),
        grid_spec=pltpu.PrefetchScalarGridSpec(
            num_scalar_prefetch=1,
            grid=(leaves // part,),
            in_specs=[pl.BlockSpec((part * rank, vecs), lambda i, p: (i, 0))]
            + [pl.BlockSpec((part,) + a.shape[1:], lambda i, p: (i, 0, 0)) for a in lhs] + [any_] * len(pieces),
            out_specs=pl.BlockSpec((part * size, vecs), lambda i, p: (i, 0)),
            scratch_shapes=[pltpu.VMEM((3 * rows + size, vecs), BF), pltpu.SemaphoreType.DMA((len(pieces),))],
        ),
        out_shape=jax.ShapeDtypeStruct((rows, vecs), BF),
        compiler_params=pltpu.CompilerParams(vmem_limit_bytes=VMEM),
        cost_estimate=cost(6),
        name="leaf_rows",
    )(pos, down, *lhs, *pieces)


def split_kernel(src, early, late, held, sems):
    jobs, at = [], 0
    for dst in (early, late):
        for start in range(0, dst.shape[0], 1536):
            size = min(1536, dst.shape[0] - start)
            jobs.append((at + start, size, dst, start))
        at += dst.shape[0]
    into = [pltpu.make_async_copy(src.at[pl.ds(a, size)], held.at[pl.ds(a, size)], sems.at[0, n])
            for n, (a, size, _, _) in enumerate(jobs)]
    back = [pltpu.make_async_copy(held.at[pl.ds(a, size)], dst.at[pl.ds(b, size)], sems.at[1, n])
            for n, (a, size, dst, b) in enumerate(jobs)]
    for c in into:
        c.start()
    for c, d in zip(into, back):
        c.wait()
        d.start()
    for d in back:
        d.wait()


def split(value, cut):
    rows, vecs = value.shape
    hbm = pl.BlockSpec(memory_space=pltpu.HBM)
    return pl.pallas_call(
        split_kernel,
        in_specs=[hbm],
        out_specs=[hbm, hbm],
        out_shape=[jax.ShapeDtypeStruct((cut, vecs), BF), jax.ShapeDtypeStruct((rows - cut, vecs), BF)],
        scratch_shapes=[pltpu.VMEM((rows, vecs), BF), pltpu.SemaphoreType.DMA((2, rows // 1536 + 3))],
        compiler_params=pltpu.CompilerParams(vmem_limit_bytes=VMEM),
        cost_estimate=cost(2),
        name="split",
    )(value)


def slots_of(ids, level, own, base, per_slab):
    slab = lax.shift_right_arithmetic(ids, level)
    inside = ids & (lax.shift_left(jnp.ones_like(level), level) - 1)
    block = jnp.where(slab == own, 0, jnp.where(slab == (own ^ 1), 1, 2))
    return jnp.where(ids >= 0, block * per_slab + base + inside, 3 * per_slab)


def after(value, *marks):
    return lax.optimization_barrier((value,) + marks)[0]


def shards(points, leaf_basis, local_transfer, top_transfer, local_coupling, local_lists,
           top_coupling, top_lists, near_blocks, near_lists):
    leaf_dev, leaf_size, rank = leaf_basis.shape
    nodes = local_transfer.shape[0]
    count = lax.axis_size("leaf")
    own = lax.axis_index("leaf")
    mates = [(i, i ^ 1) for i in range(count)]
    others = [(i, i + 1) for i in range(1, count - 1, 2)]
    others = others + [(j, i) for i, j in others]

    def swap(value, pairs):
        return lax.ppermute(value, "leaf", pairs)

    def by_xor(value, bits):
        return swap(value, [(i, i ^ bits) for i in range(count)])

    basis_t = jnp.transpose(leaf_basis, (1, 2, 0))
    transfer_t = jnp.transpose(local_transfer, (1, 2, 0))
    near_t = jnp.transpose(near_blocks, (1, 2, 3, 0))
    coup_t = jnp.transpose(local_coupling, (1, 2, 3, 0))
    near_t = jnp.transpose(near_blocks, (1, 2, 3, 0))
    coup_t = jnp.transpose(local_coupling, (1, 2, 3, 0))
    early, late = split(points, CUT * leaf_size)
    early_other = swap(early, others)
    coeff, keep, give = upward(own[None], after(points, early), basis_t, transfer_t)
    gathered = (keep + swap(give, mates)).astype(BF)
    step = 2
    while step < count:
        gathered = jnp.concatenate([gathered, by_xor(gathered, step)], axis=0)
        if step == 2:
            gathered = after(gathered, early_other)
        gathered = jnp.concatenate([gathered, by_xor(gathered, 3 * step)], axis=0)
        step *= 4
    gathered_mate = swap(gathered, mates)
    coeff_other = swap(after(coeff, gathered), others)
    coeff_mate = swap(after(coeff, gathered), mates)
    late = after(late, gathered)
    above = top(own[None], top_lists.T, gathered, gathered_mate, jnp.transpose(top_transfer, (1, 2, 0)),
                jnp.transpose(top_coupling, (1, 2, 3, 0)))
    late_other = swap(late, others)
    points_mate = swap(after(points, gathered), mates)
    lhs_coup = [turn(after(coup_t, above), transfer_t, "coupling_turn", 0, rank)]
    lhs_near = [turn(after(near_t, lhs_coup[0]), basis_t, "near_turn", 0, leaf_size)]
    above = after(above, lhs_near[0])
    leaf_log = leaf_dev.bit_length() - 1
    near_pos = slots_of(near_lists.T, jnp.full((1, leaf_dev), leaf_log, jnp.int32), own, 0, leaf_dev)
    level = np.array([[(n + 1).bit_length() - 1 for n in range(nodes)]], np.int32)
    coup_pos = slots_of(local_lists.T, jnp.asarray(level), own, jnp.asarray(2 ** level - 1 - FIRST), nodes - FIRST)
    down = downward(coup_pos, lhs_coup, coeff, coeff_mate, coeff_other, above)
    return leaf_rows(near_pos, lhs_near, down, points, points_mate, early_other, late_other)


CUT = 56


def solution(mesh):
    leaf, whole = P("leaf"), P()
    return jax.shard_map(
        shards,
        mesh=mesh,
        in_specs=(leaf, leaf, leaf, whole, leaf, leaf, whole, whole, leaf, leaf),
        out_specs=leaf,
        check_vma=False,
    )
```

```python
import jax
import jax.numpy as jnp
import numpy as np
from jax import lax
from jax.experimental import pallas as pl
from jax.experimental.pallas import tpu as pltpu
from jax.sharding import PartitionSpec as P

BF = jnp.bfloat16
F32 = jnp.float32
NT = (((1,), (1,)), ((), ()))
NN = (((1,), (0,)), ((), ()))
TN = (((0,), (0,)), ((), ()))
PAD = 8
FIRST = 7
SCALE = 40000
VMEM = 28 << 20
MOST = 50 << 20
ANY = pl.BlockSpec(memory_space=pl.ANY)


def dot(a, b, dims=NN):
    return lax.dot_general(a, b, dims, preferred_element_type=F32)


def cost(us):
    return pl.CostEstimate(flops=0, bytes_accessed=us * SCALE, transcendentals=0)


def eye(rows, cols):
    return (lax.broadcasted_iota(jnp.int32, (rows, cols), 0)
            == lax.broadcasted_iota(jnp.int32, (rows, cols), 1)).astype(BF)


def batch(count, width, load, work, store):
    width = min(width, count)

    def trip(t, carry):
        at = [t * width + u for u in range(width)]
        got = [load(i) for i in at]
        done = [work(*g) for g in got]
        for i, d in zip(at, done):
            store(i, d)
        return carry

    if count == width:
        trip(0, 0)
    else:
        lax.fori_loop(0, count // width, trip, 0)


def rows_at(index, height, many=1):
    start = index * height
    return pl.ds(start if isinstance(start, int) else pl.multiple_of(start, height), many * height)


def put(wide, at, value):
    width = value.shape[1]
    for j in range(wide.shape[0]):
        piece = value[:, j * 128:min(width, (j + 1) * 128)]
        wide[j, pl.ds(at if isinstance(at, int) else pl.multiple_of(at, 8), value.shape[0]), 0:piece.shape[1]] = piece


def turn_kernel(blocks, extra, out, wide):
    slots, rows, cols, lanes = blocks.shape
    count, _, width = out.shape
    ident = eye(count, lanes)
    step = count + PAD
    chunks = wide.shape[0]

    batch(rows, 8,
          lambda r: (jnp.concatenate([blocks[:, r].reshape(slots * cols, lanes), extra[r]], axis=0),),
          lambda both: dot(ident, both, NT),
          lambda r, turned: put(wide, r * step, turned))

    def store(i, parts):
        for j in range(chunks):
            end = min(width, (j + 1) * 128)
            out[i, :, j * 128:end] = parts[j][:, 0:end - j * 128]

    batch(count, 16,
          lambda i: [wide[j, pl.ds(i, rows, stride=step), :] for j in range(chunks)],
          lambda *parts: [p.astype(BF) for p in parts], store)


def turn(blocks_t, extra_t, name, first, rows, part=16):
    slots, _, cols, lanes = blocks_t.shape
    skip = first // part
    width = slots * cols + extra_t.shape[1]
    count = (lanes + 7) // 8 * 8
    chunks = (width + 127) // 128
    return pl.pallas_call(
        turn_kernel,
        grid=(rows // part,),
        in_specs=[pl.BlockSpec((slots, part, cols, lanes), lambda i: (0, i + skip, 0, 0)),
                  pl.BlockSpec((part,) + extra_t.shape[1:], lambda i: (i + skip, 0, 0))],
        out_specs=pl.BlockSpec((count, part, width), lambda i: (0, i, 0)),
        out_shape=jax.ShapeDtypeStruct((count, rows, width), BF),
        scratch_shapes=[pltpu.VMEM((chunks, part * (count + PAD), 128), F32)],
        compiler_params=pltpu.CompilerParams(vmem_limit_bytes=VMEM),
        cost_estimate=cost(max(1, rows * count // 1024)),
        name=name,
    )(blocks_t, extra_t)


def upward_kernel(me, points_in, basis_in, transfer_in, coeff, keep, give, late, points, basis, transfer, wide_b, wide_e, sems):
    size, rank, leaves = basis.shape
    copies = [pltpu.make_async_copy(src, dst, sems.at[n])
              for n, (src, dst) in enumerate(((basis_in, basis), (transfer_in, transfer), (points_in, points)))]
    for c in copies:
        c.start()
    nodes = transfer.shape[2]
    padded = nodes + 1
    ident = eye(leaves, leaves)
    ident_e = eye(padded, nodes)
    step_b, step_e = leaves + PAD, padded + PAD

    copies[0].wait()
    batch(size, 16, lambda p: (basis[p],), lambda b: dot(ident, b, NT), lambda p, v: put(wide_b, p * step_b, v))
    copies[1].wait()
    batch(rank, 16, lambda r: (transfer[r],), lambda b: dot(ident_e, b, NT), lambda r, v: put(wide_e, r * step_e, v))

    copies[2].wait()
    send = pltpu.make_async_copy(points.at[pl.ds(points.shape[0] - late.shape[0], late.shape[0])], late, sems.at[3])
    send.start()

    def store_leaf(leaf, got):
        coeff[rows_at(leaves - 1 + leaf, rank), :] = got

    batch(leaves, 32,
          lambda leaf: (wide_b[0, pl.ds(leaf, size, stride=step_b), :], points[rows_at(leaf, size), :]),
          lambda mine, x: dot(mine.astype(BF)[:, 0:rank], x, TN).astype(BF), store_leaf)

    def e_of(node):
        return wide_e[0, pl.ds(node, rank, stride=step_e), :]

    def pair_work(left, right, kids):
        both = jnp.concatenate([left, right], axis=0).astype(BF)[:, 0:rank]
        return dot(both, kids, TN).astype(BF)

    count = leaves // 2
    while count >= 1:
        def load(p, count=count):
            left = 2 * count - 1 + 2 * p
            return e_of(left), e_of(left + 1), coeff[rows_at(left, rank, 2), :]

        def store(p, got, count=count):
            coeff[rows_at(count - 1 + p, rank), :] = got

        batch(count, 32, load, pair_work, store)
        count //= 2
    root = dot(e_of(0).astype(BF)[:, 0:rank], coeff[0:rank, :], TN)
    low, high = root[0:rank // 2], root[rank // 2:]
    odd = (me[0] & 1) == 1
    keep[...] = jnp.where(odd, high, low)
    give[...] = jnp.where(odd, low, high)
    send.wait()
    coeff[pl.ds(nodes * rank, rank), :] = jnp.zeros((rank, coeff.shape[1]), BF)


def upward(me, points, basis_t, transfer_t, cut):
    size, rank, leaves = basis_t.shape
    padded = transfer_t.shape[2] + 1
    vecs = points.shape[1]
    return pl.pallas_call(
        upward_kernel,
        in_specs=[pl.BlockSpec(memory_space=pltpu.SMEM)] + [pl.BlockSpec(memory_space=pltpu.HBM)] * 3,
        out_shape=(jax.ShapeDtypeStruct((padded * rank, vecs), BF),)
        + (jax.ShapeDtypeStruct((rank // 2, vecs), F32),) * 2
        + (jax.ShapeDtypeStruct((points.shape[0] - cut, vecs), BF),),
        out_specs=[pl.BlockSpec(memory_space=pltpu.VMEM)] * 3 + [pl.BlockSpec(memory_space=pltpu.HBM)],
        scratch_shapes=[pltpu.VMEM(points.shape, BF), pltpu.VMEM(basis_t.shape, BF), pltpu.VMEM(transfer_t.shape, BF),
                        pltpu.VMEM((1, size * (leaves + PAD), 128), F32),
                        pltpu.VMEM((1, rank * (padded + PAD), 128), F32), pltpu.SemaphoreType.DMA((4,))],
        compiler_params=pltpu.CompilerParams(vmem_limit_bytes=MOST),
        cost_estimate=cost(7),
        name="upward",
    )(me, points, basis_t, transfer_t)


def top_kernel(where_am_i, lists, mine_in, mate_in, transfer_in, coupling_in, out, mine, mate, transfer, coupling,
               wide_e, wide_c, coeff, sems):
    rank, _, nodes = transfer.shape
    copies = [pltpu.make_async_copy(src, dst, sems.at[n]) for n, (src, dst) in enumerate(
        ((transfer_in, transfer), (mine_in, mine), (mate_in, mate), (coupling_in, coupling)))]
    for c in copies:
        c.start()
    slots = coupling.shape[0]
    chips = nodes // 2
    me = where_am_i[0]
    depths = nodes.bit_length() - 1
    step = nodes + PAD
    ident = eye(nodes, nodes)
    row = lax.broadcasted_iota(jnp.int32, (8, nodes), 0)
    lane = lax.broadcasted_iota(jnp.int32, (8, nodes), 1)
    ancestor = lax.shift_right_logical(nodes + me, jnp.maximum(depths - 2 - row, 0))
    picks = ((lane == ancestor) & (row < depths - 2)).astype(BF)

    copies[0].wait()
    batch(rank, 16, lambda r: (transfer[r],), lambda e: dot(ident, e, NT), lambda r, v: put(wide_e, r * step, v))
    coeff[0:rank, :] = jnp.zeros((rank, coeff.shape[1]), BF)

    chip = lax.shift_right_logical(me, 1)
    half = rank // 2
    copies[1].wait()
    copies[2].wait()
    for held, core in ((mine, me & 1), (mate, 1 - (me & 1))):
        def place(q, got, core=core):
            seen = chip ^ q ^ (lax.shift_right_logical(q, 1) & 0b010101)
            coeff[pl.ds(pl.multiple_of((chips + seen) * rank + core * half, half), half), :] = got

        batch(chips, 16, lambda q, held=held: (held[rows_at(q, half), :],), lambda v: v, place)

    def e_of(node):
        return wide_e[0, pl.ds(node, rank, stride=step), :]

    def pair_work(left, right, kids):
        both = jnp.concatenate([left, right], axis=0).astype(BF)[:, 0:rank]
        return dot(both, kids, TN).astype(BF)

    count = chips // 2
    while count >= 4:
        def load(p, count=count):
            left = 2 * (count + p)
            return e_of(left), e_of(left + 1), coeff[rows_at(left, rank, 2), :]

        def store(p, got, count=count):
            coeff[rows_at(count + p, rank), :] = got

        batch(count, 32, load, pair_work, store)
        count //= 2

    copies[3].wait()
    batch(rank, 16, lambda r: (coupling[:, r].reshape(slots * rank, nodes),), lambda c: dot(picks, c, NT),
          lambda r, v: put(wide_c, r * 8, v))
    fars = []
    for depth in range(2, depths):
        node = lax.shift_right_logical(nodes + me, depths - depth)
        rhs = jnp.concatenate([coeff[rows_at(jnp.maximum(lists[s, node], 0), rank), :] for s in range(slots)], axis=0)
        lhs = jnp.concatenate(
            [wide_c[j, pl.ds(depth - 2, rank, stride=8), :].astype(BF) for j in range(wide_c.shape[0])], axis=1)
        fars.append((node, dot(lhs, rhs)))
    down = None
    for node, far in fars:
        down = far if down is None else far + dot(e_of(node).astype(BF)[:, 0:rank], down.astype(BF))
    out[...] = down.astype(BF)


def top(me, lists_t, mine, mate, transfer_t, coupling_t):
    rank, _, nodes = transfer_t.shape
    vecs = mine.shape[1]
    chunks = coupling_t.shape[0] * rank // 128
    sm = pl.BlockSpec(memory_space=pltpu.SMEM)
    hbm = pl.BlockSpec(memory_space=pltpu.HBM)
    return pl.pallas_call(
        top_kernel,
        in_specs=[sm, sm, ANY, ANY, hbm, hbm],
        out_shape=jax.ShapeDtypeStruct((rank, vecs), BF),
        scratch_shapes=[pltpu.VMEM(mine.shape, BF), pltpu.VMEM(mine.shape, BF), pltpu.VMEM(transfer_t.shape, BF), pltpu.VMEM(coupling_t.shape, BF),
                        pltpu.VMEM((1, rank * (nodes + PAD), 128), F32), pltpu.VMEM((chunks, rank * 8, 128), F32),
                        pltpu.VMEM((nodes * rank, vecs), BF), pltpu.SemaphoreType.DMA((4,))],
        compiler_params=pltpu.CompilerParams(vmem_limit_bytes=VMEM),
        cost_estimate=cost(4),
        name="top",
    )(me, lists_t, mine, mate, transfer_t, coupling_t)


def down_kernel(pos, blocks_in, transfer_in, own, mate, other, above, out, blocks, transfer, window, wide, down, sems):
    slots, rank, _, nodes = blocks.shape
    leaves = (nodes + 1) // 2
    rows = (nodes - FIRST) * rank
    part = rank // PARTS
    step = nodes + 1 + PAD
    width = (slots + 1) * rank
    chunks = wide.shape[0]
    ident = eye(nodes + 1, nodes)

    load_transfer = pltpu.make_async_copy(transfer_in, transfer, sems.at[0])
    load_blocks = [pltpu.make_async_copy(blocks_in.at[:, pl.ds(p * part, part)], blocks.at[:, pl.ds(p * part, part)],
                                         sems.at[1 + p]) for p in range(PARTS)]
    load_window = [pltpu.make_async_copy(src.at[pl.ds(FIRST * rank, rows)], window.at[pl.ds(n * rows, rows)],
                                         sems.at[1 + PARTS + n]) for n, src in enumerate((own, mate, other))]
    for c in [load_transfer] + load_blocks + load_window:
        c.start()
    window[3 * rows:3 * rows + rank, :] = jnp.zeros((rank, window.shape[1]), BF)
    load_transfer.wait()
    for p in range(PARTS):
        load_blocks[p].wait()
        batch(part, 8,
              lambda r, p=p: (jnp.concatenate(
                  [blocks[:, p * part + r].reshape(slots * rank, nodes), transfer[p * part + r]], axis=0),),
              lambda both: dot(ident, both, NT),
              lambda r, turned, p=p: put(wide, (p * part + r) * step, turned))

    def parent_of(node):
        if isinstance(node, int):
            return down[rows_at((node - 1) // 2, rank), :] if node else above[...]
        return down[rows_at(lax.shift_right_logical(node - 1, 1), rank), :]

    for node in range(FIRST):
        mine = wide[chunks - 1, pl.ds(node, rank, stride=step), :].astype(BF)[:, 0:rank]
        down[rows_at(node, rank), :] = dot(mine, parent_of(node)).astype(BF)
    for c in load_window:
        c.wait()

    def work(mine, rhs):
        lhs = jnp.concatenate([m.astype(BF) for m in mine], axis=1)[:, 0:width]
        return dot(lhs, rhs).astype(BF)

    count = FIRST + 1
    while count <= leaves:
        def load(p, count=count):
            node = count - 1 + p
            return ([wide[j, pl.ds(node, rank, stride=step), :] for j in range(chunks)],
                    jnp.concatenate([window[rows_at(pos[s, node], rank), :] for s in range(slots)]
                                    + [parent_of(node)], axis=0))

        def store(p, got, count=count):
            if count == leaves:
                out[rows_at(p, rank), :] = got
            else:
                down[rows_at(count - 1 + p, rank), :] = got

        batch(count, 32, load, work, store)
        count *= 2


PARTS = 4


def downward(pos, blocks_t, transfer_t, own, mate, other, above):
    slots, rank, _, nodes = blocks_t.shape
    leaves = (nodes + 1) // 2
    vecs = own.shape[1]
    rows = (nodes - FIRST) * rank
    chunks = ((slots + 1) * rank + 127) // 128
    hbm = pl.BlockSpec(memory_space=pltpu.HBM)
    return pl.pallas_call(
        down_kernel,
        in_specs=[pl.BlockSpec(memory_space=pltpu.SMEM)] + [hbm] * 5 + [pl.BlockSpec(memory_space=pltpu.VMEM)],
        out_shape=jax.ShapeDtypeStruct((leaves * rank, vecs), BF),
        scratch_shapes=[pltpu.VMEM(blocks_t.shape, BF), pltpu.VMEM(transfer_t.shape, BF),
                        pltpu.VMEM((3 * rows + rank, vecs), BF),
                        pltpu.VMEM((chunks, rank * (nodes + 1 + PAD), 128), F32),
                        pltpu.VMEM((leaves * rank, vecs), BF), pltpu.SemaphoreType.DMA((4 + PARTS,))],
        compiler_params=pltpu.CompilerParams(vmem_limit_bytes=40 << 20),
        cost_estimate=cost(11),
        name="downward",
    )(pos, blocks_t, transfer_t, own, mate, other, above)


def rows_kernel(parts, count, pos, down, *refs):
    lhs, pieces, (out, window, sems) = refs[:parts], refs[parts:parts + count], refs[parts + count:]
    i = pl.program_id(0)
    part, _, width = lhs[0].shape
    size = sum(a.shape[1] for a in lhs)
    rank = down.shape[0] // part
    slots = (width - rank) // size

    @pl.when(i == 0)
    def _():
        copies, at = [], 0
        for n, src in enumerate(pieces):
            copies.append(pltpu.make_async_copy(src, window.at[pl.ds(at, src.shape[0])], sems.at[n]))
            at += src.shape[0]
        for c in copies:
            c.start()
        window[at:at + size, :] = jnp.zeros((size, window.shape[1]), BF)
        for c in copies:
            c.wait()

    def load(l):
        return jnp.concatenate([a[l] for a in lhs], axis=0), jnp.concatenate(
            [window[rows_at(pos[s, i * part + l], size), :] for s in range(slots)] + [down[rows_at(l, rank), :]], axis=0)

    def store(l, got):
        out[rows_at(l, size), :] = got

    batch(part, 16, load, lambda a, b: dot(a, b).astype(BF), store)


def leaf_rows(pos, lhs, down, *pieces):
    leaves, _, width = lhs[0].shape
    size = sum(a.shape[1] for a in lhs)
    rows, vecs = pieces[0].shape
    rank = down.shape[0] // leaves
    part = 32
    any_ = pl.BlockSpec(memory_space=pltpu.HBM)
    return pl.pallas_call(
        lambda *refs: rows_kernel(len(lhs), len(pieces), *refs),
        grid_spec=pltpu.PrefetchScalarGridSpec(
            num_scalar_prefetch=1,
            grid=(leaves // part,),
            in_specs=[pl.BlockSpec((part * rank, vecs), lambda i, p: (i, 0))]
            + [pl.BlockSpec((part,) + a.shape[1:], lambda i, p: (i, 0, 0)) for a in lhs] + [any_] * len(pieces),
            out_specs=pl.BlockSpec((part * size, vecs), lambda i, p: (i, 0)),
            scratch_shapes=[pltpu.VMEM((3 * rows + size, vecs), BF), pltpu.SemaphoreType.DMA((len(pieces),))],
        ),
        out_shape=jax.ShapeDtypeStruct((rows, vecs), BF),
        compiler_params=pltpu.CompilerParams(vmem_limit_bytes=VMEM),
        cost_estimate=cost(6),
        name="leaf_rows",
    )(pos, down, *lhs, *pieces)


def head_kernel(src, dst, held, sems):
    rows = dst.shape[0]
    part = rows // 4
    at = [pl.ds(n * part, part) for n in range(4)]
    into = [pltpu.make_async_copy(src.at[a], held.at[a], sems.at[0, n]) for n, a in enumerate(at)]
    back = [pltpu.make_async_copy(held.at[a], dst.at[a], sems.at[1, n]) for n, a in enumerate(at)]
    for c in into:
        c.start()
    for c, d in zip(into, back):
        c.wait()
        d.start()
    for d in back:
        d.wait()


def head(value, rows):
    vecs = value.shape[1]
    hbm = pl.BlockSpec(memory_space=pltpu.HBM)
    return pl.pallas_call(
        head_kernel,
        in_specs=[hbm],
        out_specs=hbm,
        out_shape=jax.ShapeDtypeStruct((rows, vecs), BF),
        scratch_shapes=[pltpu.VMEM((rows, vecs), BF), pltpu.SemaphoreType.DMA((2, 4))],
        compiler_params=pltpu.CompilerParams(vmem_limit_bytes=MOST),
        cost_estimate=cost(2),
        name="head",
    )(value)


def slots_of(ids, level, own, base, per_slab):
    slab = lax.shift_right_arithmetic(ids, level)
    inside = ids & (lax.shift_left(jnp.ones_like(level), level) - 1)
    block = jnp.where(slab == own, 0, jnp.where(slab == (own ^ 1), 1, 2))
    return jnp.where(ids >= 0, block * per_slab + base + inside, 3 * per_slab)


def after(value, *marks):
    return lax.optimization_barrier((value,) + marks)[0]


def shards(points, leaf_basis, local_transfer, top_transfer, local_coupling, local_lists,
           top_coupling, top_lists, near_blocks, near_lists):
    leaf_dev, leaf_size, rank = leaf_basis.shape
    nodes = local_transfer.shape[0]
    count = lax.axis_size("leaf")
    own = lax.axis_index("leaf")
    mates = [(i, i ^ 1) for i in range(count)]
    others = [(i, i + 1) for i in range(1, count - 1, 2)]
    others = others + [(j, i) for i, j in others]

    def swap(value, pairs):
        return lax.ppermute(value, "leaf", pairs)

    def by_xor(value, bits):
        return swap(value, [(i, i ^ bits) for i in range(count)])

    basis_t = jnp.transpose(leaf_basis, (1, 2, 0))
    transfer_t = jnp.transpose(local_transfer, (1, 2, 0))
    near_t = jnp.transpose(near_blocks, (1, 2, 3, 0))
    coup_t = jnp.transpose(local_coupling, (1, 2, 3, 0))
    near_t = jnp.transpose(near_blocks, (1, 2, 3, 0))
    coup_t = jnp.transpose(local_coupling, (1, 2, 3, 0))
    cut = CUT * leaf_size
    early = head(points, cut)
    early_other = swap(early, others)
    coeff, keep, give, late = upward(own[None], after(points, early), basis_t, transfer_t, cut)
    gathered = (keep + swap(give, mates)).astype(BF)
    leaf_log = leaf_dev.bit_length() - 1
    near_pos = slots_of(near_lists.T, jnp.full((1, leaf_dev), leaf_log, jnp.int32), own, 0, leaf_dev)
    level = np.array([[(n + 1).bit_length() - 1 for n in range(nodes)]], np.int32)
    coup_pos = slots_of(local_lists.T, jnp.asarray(level), own, jnp.asarray(2 ** level - 1 - FIRST), nodes - FIRST)
    step = 2
    while step < count:
        came = [by_xor(gathered, way * step) for way in (1, 3, 2)]
        gathered = jnp.concatenate([gathered] + came, axis=0)
        if step == 2:
            gathered = after(gathered, early_other, near_pos, coup_pos)
        step *= 4
    gathered_mate = swap(gathered, mates)
    coeff_other = swap(after(coeff, came[0]), others)
    above = top(own[None], top_lists.T, gathered, gathered_mate, jnp.transpose(top_transfer, (1, 2, 0)),
                jnp.transpose(top_coupling, (1, 2, 3, 0)))
    late_other = swap(after(late, above), others)
    coeff_mate = swap(after(coeff, above), mates)
    points_mate = swap(after(points, above), mates)
    lhs_near = [turn(after(near_t, above), basis_t, "near_turn", 0, leaf_size)]
    above = after(above, lhs_near[0])
    down = downward(coup_pos, coup_t, transfer_t, coeff, coeff_mate, coeff_other, above)
    return leaf_rows(near_pos, lhs_near, down, points, points_mate, early_other, late_other)


CUT = 72


def solution(mesh):
    leaf, whole = P("leaf"), P()
    return jax.shard_map(
        shards,
        mesh=mesh,
        in_specs=(leaf, leaf, leaf, whole, leaf, leaf, whole, whole, leaf, leaf),
        out_specs=leaf,
        check_vma=False,
    )
```

```python
import jax
import jax.numpy as jnp
import numpy as np
from jax import lax
from jax.experimental import pallas as pl
from jax.experimental.pallas import tpu as pltpu
from jax.sharding import PartitionSpec as P

BF = jnp.bfloat16
F32 = jnp.float32
NT = (((1,), (1,)), ((), ()))
NN = (((1,), (0,)), ((), ()))
TN = (((0,), (0,)), ((), ()))
PAD = 8
FIRST = 7
SCALE = 40000
VMEM = 28 << 20
MOST = 50 << 20
ANY = pl.BlockSpec(memory_space=pl.ANY)


def dot(a, b, dims=NN):
    return lax.dot_general(a, b, dims, preferred_element_type=F32)


def cost(us):
    return pl.CostEstimate(flops=0, bytes_accessed=us * SCALE, transcendentals=0)


def eye(rows, cols):
    return (lax.broadcasted_iota(jnp.int32, (rows, cols), 0)
            == lax.broadcasted_iota(jnp.int32, (rows, cols), 1)).astype(BF)


def batch(count, width, load, work, store):
    width = min(width, count)

    def trip(t, carry):
        at = [t * width + u for u in range(width)]
        got = [load(i) for i in at]
        done = [work(*g) for g in got]
        for i, d in zip(at, done):
            store(i, d)
        return carry

    if count == width:
        trip(0, 0)
    else:
        lax.fori_loop(0, count // width, trip, 0)


def rows_at(index, height, many=1):
    start = index * height
    return pl.ds(start if isinstance(start, int) else pl.multiple_of(start, height), many * height)


def put(wide, at, value):
    width = value.shape[1]
    for j in range(wide.shape[0]):
        piece = value[:, j * 128:min(width, (j + 1) * 128)]
        wide[j, pl.ds(at if isinstance(at, int) else pl.multiple_of(at, 8), value.shape[0]), 0:piece.shape[1]] = piece


def turn_kernel(blocks, extra, out, wide):
    slots, rows, cols, lanes = blocks.shape
    count, _, width = out.shape
    ident = eye(count, lanes)
    step = count + PAD
    chunks = wide.shape[0]

    batch(rows, 8,
          lambda r: (jnp.concatenate([blocks[:, r].reshape(slots * cols, lanes), extra[r]], axis=0),),
          lambda both: dot(ident, both, NT),
          lambda r, turned: put(wide, r * step, turned))

    def store(i, parts):
        for j in range(chunks):
            end = min(width, (j + 1) * 128)
            out[i, :, j * 128:end] = parts[j][:, 0:end - j * 128]

    batch(count, 16,
          lambda i: [wide[j, pl.ds(i, rows, stride=step), :] for j in range(chunks)],
          lambda *parts: [p.astype(BF) for p in parts], store)


def turn(blocks_t, extra_t, name, first, rows, part=16):
    slots, _, cols, lanes = blocks_t.shape
    skip = first // part
    width = slots * cols + extra_t.shape[1]
    count = (lanes + 7) // 8 * 8
    chunks = (width + 127) // 128
    return pl.pallas_call(
        turn_kernel,
        grid=(rows // part,),
        in_specs=[pl.BlockSpec((slots, part, cols, lanes), lambda i: (0, i + skip, 0, 0)),
                  pl.BlockSpec((part,) + extra_t.shape[1:], lambda i: (i + skip, 0, 0))],
        out_specs=pl.BlockSpec((count, part, width), lambda i: (0, i, 0)),
        out_shape=jax.ShapeDtypeStruct((count, rows, width), BF),
        scratch_shapes=[pltpu.VMEM((chunks, part * (count + PAD), 128), F32)],
        compiler_params=pltpu.CompilerParams(vmem_limit_bytes=VMEM),
        cost_estimate=cost(max(1, rows * count // 1024)),
        name=name,
    )(blocks_t, extra_t)


def upward_kernel(me, points_in, basis_in, transfer_in, coeff, keep, give, late, points, basis, transfer, wide_b, wide_e, sems):
    size, rank, leaves = basis.shape
    copies = [pltpu.make_async_copy(src, dst, sems.at[n])
              for n, (src, dst) in enumerate(((basis_in, basis), (transfer_in, transfer), (points_in, points)))]
    for c in copies:
        c.start()
    nodes = transfer.shape[2]
    padded = nodes + 1
    ident = eye(leaves, leaves)
    ident_e = eye(padded, nodes)
    step_b, step_e = leaves + PAD, padded + PAD

    copies[0].wait()
    batch(size, 16, lambda p: (basis[p],), lambda b: dot(ident, b, NT), lambda p, v: put(wide_b, p * step_b, v))
    copies[1].wait()
    batch(rank, 16, lambda r: (transfer[r],), lambda b: dot(ident_e, b, NT), lambda r, v: put(wide_e, r * step_e, v))

    copies[2].wait()
    send = pltpu.make_async_copy(points.at[pl.ds(points.shape[0] - late.shape[0], late.shape[0])], late, sems.at[3])
    send.start()

    def store_leaf(leaf, got):
        coeff[rows_at(leaves - 1 + leaf, rank), :] = got

    batch(leaves, 32,
          lambda leaf: (wide_b[0, pl.ds(leaf, size, stride=step_b), :], points[rows_at(leaf, size), :]),
          lambda mine, x: dot(mine.astype(BF)[:, 0:rank], x, TN).astype(BF), store_leaf)

    def e_of(node):
        return wide_e[0, pl.ds(node, rank, stride=step_e), :]

    def pair_work(left, right, kids):
        both = jnp.concatenate([left, right], axis=0).astype(BF)[:, 0:rank]
        return dot(both, kids, TN).astype(BF)

    count = leaves // 2
    while count >= 1:
        def load(p, count=count):
            left = 2 * count - 1 + 2 * p
            return e_of(left), e_of(left + 1), coeff[rows_at(left, rank, 2), :]

        def store(p, got, count=count):
            coeff[rows_at(count - 1 + p, rank), :] = got

        batch(count, 32, load, pair_work, store)
        count //= 2
    root = dot(e_of(0).astype(BF)[:, 0:rank], coeff[0:rank, :], TN)
    low, high = root[0:rank // 2], root[rank // 2:]
    odd = (me[0] & 1) == 1
    keep[...] = jnp.where(odd, high, low)
    give[...] = jnp.where(odd, low, high)
    send.wait()
    coeff[pl.ds(nodes * rank, rank), :] = jnp.zeros((rank, coeff.shape[1]), BF)


def upward(me, points, basis_t, transfer_t, cut):
    size, rank, leaves = basis_t.shape
    padded = transfer_t.shape[2] + 1
    vecs = points.shape[1]
    return pl.pallas_call(
        upward_kernel,
        in_specs=[pl.BlockSpec(memory_space=pltpu.SMEM)] + [pl.BlockSpec(memory_space=pltpu.HBM)] * 3,
        out_shape=(jax.ShapeDtypeStruct((padded * rank, vecs), BF),)
        + (jax.ShapeDtypeStruct((rank // 2, vecs), F32),) * 2
        + (jax.ShapeDtypeStruct((points.shape[0] - cut, vecs), BF),),
        out_specs=[pl.BlockSpec(memory_space=pltpu.VMEM)] * 3 + [pl.BlockSpec(memory_space=pltpu.HBM)],
        scratch_shapes=[pltpu.VMEM(points.shape, BF), pltpu.VMEM(basis_t.shape, BF), pltpu.VMEM(transfer_t.shape, BF),
                        pltpu.VMEM((1, size * (leaves + PAD), 128), F32),
                        pltpu.VMEM((1, rank * (padded + PAD), 128), F32), pltpu.SemaphoreType.DMA((4,))],
        compiler_params=pltpu.CompilerParams(vmem_limit_bytes=MOST),
        cost_estimate=cost(7),
        name="upward",
    )(me, points, basis_t, transfer_t)


def top_kernel(where_am_i, lists, mine_in, mate_in, transfer_in, coupling_in, out, mine, mate, transfer, coupling,
               wide_e, wide_c, coeff, sems):
    rank, _, nodes = transfer.shape
    copies = [pltpu.make_async_copy(src, dst, sems.at[n]) for n, (src, dst) in enumerate(
        ((transfer_in, transfer), (mine_in, mine), (mate_in, mate), (coupling_in, coupling)))]
    for c in copies:
        c.start()
    slots = coupling.shape[0]
    chips = nodes // 2
    me = where_am_i[0]
    depths = nodes.bit_length() - 1
    step = nodes + PAD
    ident = eye(nodes, nodes)
    row = lax.broadcasted_iota(jnp.int32, (8, nodes), 0)
    lane = lax.broadcasted_iota(jnp.int32, (8, nodes), 1)
    ancestor = lax.shift_right_logical(nodes + me, jnp.maximum(depths - 2 - row, 0))
    picks = ((lane == ancestor) & (row < depths - 2)).astype(BF)

    copies[0].wait()
    batch(rank, 16, lambda r: (transfer[r],), lambda e: dot(ident, e, NT), lambda r, v: put(wide_e, r * step, v))
    coeff[0:rank, :] = jnp.zeros((rank, coeff.shape[1]), BF)

    chip = lax.shift_right_logical(me, 1)
    half = rank // 2
    copies[1].wait()
    copies[2].wait()
    for held, core in ((mine, me & 1), (mate, 1 - (me & 1))):
        def place(q, got, core=core):
            seen = chip ^ q ^ (lax.shift_right_logical(q, 1) & 0b010101)
            coeff[pl.ds(pl.multiple_of((chips + seen) * rank + core * half, half), half), :] = got

        batch(chips, 16, lambda q, held=held: (held[rows_at(q, half), :],), lambda v: v, place)

    def e_of(node):
        return wide_e[0, pl.ds(node, rank, stride=step), :]

    def pair_work(left, right, kids):
        both = jnp.concatenate([left, right], axis=0).astype(BF)[:, 0:rank]
        return dot(both, kids, TN).astype(BF)

    count = chips // 2
    while count >= 4:
        def load(p, count=count):
            left = 2 * (count + p)
            return e_of(left), e_of(left + 1), coeff[rows_at(left, rank, 2), :]

        def store(p, got, count=count):
            coeff[rows_at(count + p, rank), :] = got

        batch(count, 32, load, pair_work, store)
        count //= 2

    copies[3].wait()
    batch(rank, 16, lambda r: (coupling[:, r].reshape(slots * rank, nodes),), lambda c: dot(picks, c, NT),
          lambda r, v: put(wide_c, r * 8, v))
    fars = []
    for depth in range(2, depths):
        node = lax.shift_right_logical(nodes + me, depths - depth)
        rhs = jnp.concatenate([coeff[rows_at(jnp.maximum(lists[s, node], 0), rank), :] for s in range(slots)], axis=0)
        lhs = jnp.concatenate(
            [wide_c[j, pl.ds(depth - 2, rank, stride=8), :].astype(BF) for j in range(wide_c.shape[0])], axis=1)
        fars.append((node, dot(lhs, rhs)))
    down = None
    for node, far in fars:
        down = far if down is None else far + dot(e_of(node).astype(BF)[:, 0:rank], down.astype(BF))
    out[...] = down.astype(BF)


def top(me, lists_t, mine, mate, transfer_t, coupling_t):
    rank, _, nodes = transfer_t.shape
    vecs = mine.shape[1]
    chunks = coupling_t.shape[0] * rank // 128
    sm = pl.BlockSpec(memory_space=pltpu.SMEM)
    hbm = pl.BlockSpec(memory_space=pltpu.HBM)
    return pl.pallas_call(
        top_kernel,
        in_specs=[sm, sm, ANY, ANY, hbm, hbm],
        out_shape=jax.ShapeDtypeStruct((rank, vecs), BF),
        scratch_shapes=[pltpu.VMEM(mine.shape, BF), pltpu.VMEM(mine.shape, BF), pltpu.VMEM(transfer_t.shape, BF), pltpu.VMEM(coupling_t.shape, BF),
                        pltpu.VMEM((1, rank * (nodes + PAD), 128), F32), pltpu.VMEM((chunks, rank * 8, 128), F32),
                        pltpu.VMEM((nodes * rank, vecs), BF), pltpu.SemaphoreType.DMA((4,))],
        compiler_params=pltpu.CompilerParams(vmem_limit_bytes=VMEM),
        cost_estimate=cost(4),
        name="top",
    )(me, lists_t, mine, mate, transfer_t, coupling_t)


def down_kernel(pos, blocks_in, transfer_in, own, mate, other, above, out, blocks, transfer, window, wide, down, sems):
    slots, rank, _, nodes = blocks.shape
    leaves = (nodes + 1) // 2
    rows = (nodes - FIRST) * rank
    part = rank // PARTS
    step = nodes + 1 + PAD
    width = (slots + 1) * rank
    chunks = wide.shape[0]
    ident = eye(nodes + 1, nodes)

    load_transfer = pltpu.make_async_copy(transfer_in, transfer, sems.at[0])
    load_blocks = [pltpu.make_async_copy(blocks_in.at[:, pl.ds(p * part, part)], blocks.at[:, pl.ds(p * part, part)],
                                         sems.at[1 + p]) for p in range(PARTS)]
    load_window = [pltpu.make_async_copy(src.at[pl.ds(FIRST * rank, rows)], window.at[pl.ds(n * rows, rows)],
                                         sems.at[1 + PARTS + n]) for n, src in enumerate((own, mate, other))]
    for c in [load_transfer] + load_blocks + load_window:
        c.start()
    window[3 * rows:3 * rows + rank, :] = jnp.zeros((rank, window.shape[1]), BF)
    load_transfer.wait()
    for p in range(PARTS):
        load_blocks[p].wait()
        batch(part, 8,
              lambda r, p=p: (jnp.concatenate(
                  [blocks[:, p * part + r].reshape(slots * rank, nodes), transfer[p * part + r]], axis=0),),
              lambda both: dot(ident, both, NT),
              lambda r, turned, p=p: put(wide, (p * part + r) * step, turned))

    def parent_of(node):
        if isinstance(node, int):
            return down[rows_at((node - 1) // 2, rank), :] if node else above[...]
        return down[rows_at(lax.shift_right_logical(node - 1, 1), rank), :]

    for node in range(FIRST):
        mine = wide[chunks - 1, pl.ds(node, rank, stride=step), :].astype(BF)[:, 0:rank]
        down[rows_at(node, rank), :] = dot(mine, parent_of(node)).astype(BF)
    for c in load_window:
        c.wait()

    def work(mine, rhs):
        lhs = jnp.concatenate([m.astype(BF) for m in mine], axis=1)[:, 0:width]
        return dot(lhs, rhs).astype(BF)

    count = FIRST + 1
    while count <= leaves:
        def load(p, count=count):
            node = count - 1 + p
            return ([wide[j, pl.ds(node, rank, stride=step), :] for j in range(chunks)],
                    jnp.concatenate([window[rows_at(pos[s, node], rank), :] for s in range(slots)]
                                    + [parent_of(node)], axis=0))

        def store(p, got, count=count):
            if count == leaves:
                out[rows_at(p, rank), :] = got
            else:
                down[rows_at(count - 1 + p, rank), :] = got

        batch(count, 64, load, work, store)
        count *= 2


PARTS = 4


def downward(pos, blocks_t, transfer_t, own, mate, other, above):
    slots, rank, _, nodes = blocks_t.shape
    leaves = (nodes + 1) // 2
    vecs = own.shape[1]
    rows = (nodes - FIRST) * rank
    chunks = ((slots + 1) * rank + 127) // 128
    hbm = pl.BlockSpec(memory_space=pltpu.HBM)
    return pl.pallas_call(
        down_kernel,
        in_specs=[pl.BlockSpec(memory_space=pltpu.SMEM)] + [hbm] * 2 + [ANY] * 3 + [pl.BlockSpec(memory_space=pltpu.VMEM)],
        out_shape=jax.ShapeDtypeStruct((leaves * rank, vecs), BF),
        scratch_shapes=[pltpu.VMEM(blocks_t.shape, BF), pltpu.VMEM(transfer_t.shape, BF),
                        pltpu.VMEM((3 * rows + rank, vecs), BF),
                        pltpu.VMEM((chunks, rank * (nodes + 1 + PAD), 128), F32),
                        pltpu.VMEM((leaves * rank, vecs), BF), pltpu.SemaphoreType.DMA((4 + PARTS,))],
        compiler_params=pltpu.CompilerParams(vmem_limit_bytes=40 << 20),
        cost_estimate=cost(11),
        name="downward",
    )(pos, blocks_t, transfer_t, own, mate, other, above)


def rows_kernel(parts, count, pos, down, *refs):
    lhs, pieces, (out, window, sems) = refs[:parts], refs[parts:parts + count], refs[parts + count:]
    i = pl.program_id(0)
    part, _, width = lhs[0].shape
    size = sum(a.shape[1] for a in lhs)
    rank = down.shape[0] // part
    slots = (width - rank) // size

    @pl.when(i == 0)
    def _():
        copies, at = [], 0
        for n, src in enumerate(pieces):
            copies.append(pltpu.make_async_copy(src, window.at[pl.ds(at, src.shape[0])], sems.at[n]))
            at += src.shape[0]
        for c in copies:
            c.start()
        window[at:at + size, :] = jnp.zeros((size, window.shape[1]), BF)
        for c in copies:
            c.wait()

    def load(l):
        return jnp.concatenate([a[l] for a in lhs], axis=0), jnp.concatenate(
            [window[rows_at(pos[s, i * part + l], size), :] for s in range(slots)] + [down[rows_at(l, rank), :]], axis=0)

    def store(l, got):
        out[rows_at(l, size), :] = got

    batch(part, 16, load, lambda a, b: dot(a, b).astype(BF), store)


def leaf_rows(pos, lhs, down, *pieces):
    leaves, _, width = lhs[0].shape
    size = sum(a.shape[1] for a in lhs)
    rows, vecs = pieces[0].shape
    rank = down.shape[0] // leaves
    part = 32
    any_ = pl.BlockSpec(memory_space=pl.ANY)
    return pl.pallas_call(
        lambda *refs: rows_kernel(len(lhs), len(pieces), *refs),
        grid_spec=pltpu.PrefetchScalarGridSpec(
            num_scalar_prefetch=1,
            grid=(leaves // part,),
            in_specs=[pl.BlockSpec((part * rank, vecs), lambda i, p: (i, 0))]
            + [pl.BlockSpec((part,) + a.shape[1:], lambda i, p: (i, 0, 0)) for a in lhs] + [any_] * len(pieces),
            out_specs=pl.BlockSpec((part * size, vecs), lambda i, p: (i, 0)),
            scratch_shapes=[pltpu.VMEM((3 * rows + size, vecs), BF), pltpu.SemaphoreType.DMA((len(pieces),))],
        ),
        out_shape=jax.ShapeDtypeStruct((rows, vecs), BF),
        compiler_params=pltpu.CompilerParams(vmem_limit_bytes=VMEM),
        cost_estimate=cost(6),
        name="leaf_rows",
    )(pos, down, *lhs, *pieces)


def head_kernel(src, dst, held, sems):
    rows = dst.shape[0]
    part = rows // 4
    at = [pl.ds(n * part, part) for n in range(4)]
    into = [pltpu.make_async_copy(src.at[a], held.at[a], sems.at[0, n]) for n, a in enumerate(at)]
    back = [pltpu.make_async_copy(held.at[a], dst.at[a], sems.at[1, n]) for n, a in enumerate(at)]
    for c in into:
        c.start()
    for c, d in zip(into, back):
        c.wait()
        d.start()
    for d in back:
        d.wait()


def head(value, rows):
    vecs = value.shape[1]
    hbm = pl.BlockSpec(memory_space=pltpu.HBM)
    return pl.pallas_call(
        head_kernel,
        in_specs=[hbm],
        out_specs=hbm,
        out_shape=jax.ShapeDtypeStruct((rows, vecs), BF),
        scratch_shapes=[pltpu.VMEM((rows, vecs), BF), pltpu.SemaphoreType.DMA((2, 4))],
        compiler_params=pltpu.CompilerParams(vmem_limit_bytes=MOST),
        cost_estimate=cost(2),
        name="head",
    )(value)


def slots_of(ids, level, own, base, per_slab):
    slab = lax.shift_right_arithmetic(ids, level)
    inside = ids & (lax.shift_left(jnp.ones_like(level), level) - 1)
    block = jnp.where(slab == own, 0, jnp.where(slab == (own ^ 1), 1, 2))
    return jnp.where(ids >= 0, block * per_slab + base + inside, 3 * per_slab)


def after(value, *marks):
    return lax.optimization_barrier((value,) + marks)[0]


def shards(points, leaf_basis, local_transfer, top_transfer, local_coupling, local_lists,
           top_coupling, top_lists, near_blocks, near_lists):
    leaf_dev, leaf_size, rank = leaf_basis.shape
    nodes = local_transfer.shape[0]
    count = lax.axis_size("leaf")
    own = lax.axis_index("leaf")
    mates = [(i, i ^ 1) for i in range(count)]
    others = [(i, i + 1) for i in range(1, count - 1, 2)]
    others = others + [(j, i) for i, j in others]

    def swap(value, pairs):
        return lax.ppermute(value, "leaf", pairs)

    def by_xor(value, bits):
        return swap(value, [(i, i ^ bits) for i in range(count)])

    basis_t = jnp.transpose(leaf_basis, (1, 2, 0))
    transfer_t = jnp.transpose(local_transfer, (1, 2, 0))
    near_t = jnp.transpose(near_blocks, (1, 2, 3, 0))
    coup_t = jnp.transpose(local_coupling, (1, 2, 3, 0))
    near_t = jnp.transpose(near_blocks, (1, 2, 3, 0))
    coup_t = jnp.transpose(local_coupling, (1, 2, 3, 0))
    cut = CUT * leaf_size
    early = head(points, cut)
    early_other = swap(early, others)
    coeff, keep, give, late = upward(own[None], after(points, early), basis_t, transfer_t, cut)
    gathered = (keep + swap(give, mates)).astype(BF)
    leaf_log = leaf_dev.bit_length() - 1
    near_pos = slots_of(near_lists.T, jnp.full((1, leaf_dev), leaf_log, jnp.int32), own, 0, leaf_dev)
    level = np.array([[(n + 1).bit_length() - 1 for n in range(nodes)]], np.int32)
    coup_pos = slots_of(local_lists.T, jnp.asarray(level), own, jnp.asarray(2 ** level - 1 - FIRST), nodes - FIRST)
    step = 2
    while step < count:
        came = [by_xor(gathered, way * step) for way in (1, 3, 2)]
        gathered = jnp.concatenate([gathered] + came, axis=0)
        if step == 2:
            gathered = after(gathered, early_other, near_pos, coup_pos)
        step *= 4
    gathered_mate = swap(gathered, mates)
    coeff_other = swap(after(coeff, came[0]), others)
    above = top(own[None], top_lists.T, gathered, gathered_mate, jnp.transpose(top_transfer, (1, 2, 0)),
                jnp.transpose(top_coupling, (1, 2, 3, 0)))
    late_other = swap(after(late, above), others)
    coeff_mate = swap(after(coeff, above), mates)
    points_mate = swap(after(points, above), mates)
    lhs_near = [turn(after(near_t, above), basis_t, "near_turn", 0, leaf_size)]
    above = after(above, lhs_near[0])
    down = downward(coup_pos, coup_t, transfer_t, coeff, coeff_mate, coeff_other, above)
    return leaf_rows(near_pos, lhs_near, down, points, points_mate, early_other, late_other)


CUT = 72


def solution(mesh):
    leaf, whole = P("leaf"), P()
    return jax.shard_map(
        shards,
        mesh=mesh,
        in_specs=(leaf, leaf, leaf, whole, leaf, leaf, whole, whole, leaf, leaf),
        out_specs=leaf,
        check_vma=False,
    )
```

```python
import jax
import jax.numpy as jnp
import numpy as np
from jax import lax
from jax.experimental import pallas as pl
from jax.experimental.pallas import tpu as pltpu
from jax.sharding import PartitionSpec as P

BF = jnp.bfloat16
F32 = jnp.float32
NT = (((1,), (1,)), ((), ()))
NN = (((1,), (0,)), ((), ()))
TN = (((0,), (0,)), ((), ()))
PAD = 8
FIRST = 7
SCALE = 40000
VMEM = 28 << 20
MOST = 50 << 20
ANY = pl.BlockSpec(memory_space=pl.ANY)


def dot(a, b, dims=NN):
    return lax.dot_general(a, b, dims, preferred_element_type=F32)


def cost(us):
    return pl.CostEstimate(flops=0, bytes_accessed=us * SCALE, transcendentals=0)


def eye(rows, cols):
    return (lax.broadcasted_iota(jnp.int32, (rows, cols), 0)
            == lax.broadcasted_iota(jnp.int32, (rows, cols), 1)).astype(BF)


def batch(count, width, load, work, store):
    width = min(width, count)

    def trip(t, carry):
        at = [t * width + u for u in range(width)]
        got = [load(i) for i in at]
        done = [work(*g) for g in got]
        for i, d in zip(at, done):
            store(i, d)
        return carry

    if count == width:
        trip(0, 0)
    else:
        lax.fori_loop(0, count // width, trip, 0)


def rows_at(index, height, many=1):
    start = index * height
    return pl.ds(start if isinstance(start, int) else pl.multiple_of(start, height), many * height)


def put(wide, at, value):
    width = value.shape[1]
    for j in range(wide.shape[0]):
        piece = value[:, j * 128:min(width, (j + 1) * 128)]
        wide[j, pl.ds(at if isinstance(at, int) else pl.multiple_of(at, 8), value.shape[0]), 0:piece.shape[1]] = piece


def turn_kernel(blocks, extra, out, wide):
    slots, rows, cols, lanes = blocks.shape
    count, _, width = out.shape
    ident = eye(count, lanes)
    step = count + PAD
    chunks = wide.shape[0]

    batch(rows, 8,
          lambda r: (jnp.concatenate([blocks[:, r].reshape(slots * cols, lanes), extra[r]], axis=0),),
          lambda both: dot(ident, both, NT),
          lambda r, turned: put(wide, r * step, turned))

    def store(i, parts):
        for j in range(chunks):
            end = min(width, (j + 1) * 128)
            out[i, :, j * 128:end] = parts[j][:, 0:end - j * 128]

    batch(count, 16,
          lambda i: [wide[j, pl.ds(i, rows, stride=step), :] for j in range(chunks)],
          lambda *parts: [p.astype(BF) for p in parts], store)


def turn(blocks_t, extra_t, name, first, rows, part=16):
    slots, _, cols, lanes = blocks_t.shape
    skip = first // part
    width = slots * cols + extra_t.shape[1]
    count = (lanes + 7) // 8 * 8
    chunks = (width + 127) // 128
    return pl.pallas_call(
        turn_kernel,
        grid=(rows // part,),
        in_specs=[pl.BlockSpec((slots, part, cols, lanes), lambda i: (0, i + skip, 0, 0)),
                  pl.BlockSpec((part,) + extra_t.shape[1:], lambda i: (i + skip, 0, 0))],
        out_specs=pl.BlockSpec((count, part, width), lambda i: (0, i, 0)),
        out_shape=jax.ShapeDtypeStruct((count, rows, width), BF),
        scratch_shapes=[pltpu.VMEM((chunks, part * (count + PAD), 128), F32)],
        compiler_params=pltpu.CompilerParams(vmem_limit_bytes=VMEM),
        cost_estimate=cost(max(1, rows * count // 1024)),
        name=name,
    )(blocks_t, extra_t)


def upward_kernel(me, points_in, basis_in, transfer_in, coeff, keep, give, late, points, basis, transfer, wide_b, wide_e, sems):
    size, rank, leaves = basis.shape
    copies = [pltpu.make_async_copy(src, dst, sems.at[n])
              for n, (src, dst) in enumerate(((basis_in, basis), (transfer_in, transfer), (points_in, points)))]
    for c in copies:
        c.start()
    nodes = transfer.shape[2]
    padded = nodes + 1
    ident = eye(leaves, leaves)
    ident_e = eye(padded, nodes)
    step_b, step_e = leaves + PAD, padded + PAD

    copies[0].wait()
    batch(size, 16, lambda p: (basis[p],), lambda b: dot(ident, b, NT), lambda p, v: put(wide_b, p * step_b, v))
    copies[1].wait()
    batch(rank, 16, lambda r: (transfer[r],), lambda b: dot(ident_e, b, NT), lambda r, v: put(wide_e, r * step_e, v))

    copies[2].wait()
    send = pltpu.make_async_copy(points.at[pl.ds(points.shape[0] - late.shape[0], late.shape[0])], late, sems.at[3])
    send.start()

    def store_leaf(leaf, got):
        coeff[rows_at(leaves - 1 + leaf, rank), :] = got

    batch(leaves, 32,
          lambda leaf: (wide_b[0, pl.ds(leaf, size, stride=step_b), :], points[rows_at(leaf, size), :]),
          lambda mine, x: dot(mine.astype(BF)[:, 0:rank], x, TN).astype(BF), store_leaf)

    def e_of(node):
        return wide_e[0, pl.ds(node, rank, stride=step_e), :]

    def pair_work(left, right, kids):
        both = jnp.concatenate([left, right], axis=0).astype(BF)[:, 0:rank]
        return dot(both, kids, TN).astype(BF)

    count = leaves // 2
    while count >= 1:
        def load(p, count=count):
            left = 2 * count - 1 + 2 * p
            return e_of(left), e_of(left + 1), coeff[rows_at(left, rank, 2), :]

        def store(p, got, count=count):
            coeff[rows_at(count - 1 + p, rank), :] = got

        batch(count, 32, load, pair_work, store)
        count //= 2
    root = dot(e_of(0).astype(BF)[:, 0:rank], coeff[0:rank, :], TN)
    low, high = root[0:rank // 2], root[rank // 2:]
    odd = (me[0] & 1) == 1
    keep[...] = jnp.where(odd, high, low)
    give[...] = jnp.where(odd, low, high)
    send.wait()
    coeff[pl.ds(nodes * rank, rank), :] = jnp.zeros((rank, coeff.shape[1]), BF)


def upward(me, points, basis_t, transfer_t, cut):
    size, rank, leaves = basis_t.shape
    padded = transfer_t.shape[2] + 1
    vecs = points.shape[1]
    return pl.pallas_call(
        upward_kernel,
        in_specs=[pl.BlockSpec(memory_space=pltpu.SMEM)] + [pl.BlockSpec(memory_space=pltpu.HBM)] * 3,
        out_shape=(jax.ShapeDtypeStruct((padded * rank, vecs), BF),)
        + (jax.ShapeDtypeStruct((rank // 2, vecs), F32),) * 2
        + (jax.ShapeDtypeStruct((points.shape[0] - cut, vecs), BF),),
        out_specs=[pl.BlockSpec(memory_space=pltpu.VMEM)] * 3 + [pl.BlockSpec(memory_space=pltpu.HBM)],
        scratch_shapes=[pltpu.VMEM(points.shape, BF), pltpu.VMEM(basis_t.shape, BF), pltpu.VMEM(transfer_t.shape, BF),
                        pltpu.VMEM((1, size * (leaves + PAD), 128), F32),
                        pltpu.VMEM((1, rank * (padded + PAD), 128), F32), pltpu.SemaphoreType.DMA((4,))],
        compiler_params=pltpu.CompilerParams(vmem_limit_bytes=MOST),
        cost_estimate=cost(7),
        name="upward",
    )(me, points, basis_t, transfer_t)


def top_kernel(where_am_i, lists, mine_in, mate_in, transfer_in, coupling_in, out, mine, mate, transfer, coupling,
               wide_e, wide_c, coeff, sems):
    rank, _, nodes = transfer.shape
    copies = [pltpu.make_async_copy(src, dst, sems.at[n]) for n, (src, dst) in enumerate(
        ((transfer_in, transfer), (mine_in, mine), (mate_in, mate), (coupling_in, coupling)))]
    for c in copies:
        c.start()
    slots = coupling.shape[0]
    chips = nodes // 2
    me = where_am_i[0]
    depths = nodes.bit_length() - 1
    step = nodes + PAD
    ident = eye(nodes, nodes)
    row = lax.broadcasted_iota(jnp.int32, (8, nodes), 0)
    lane = lax.broadcasted_iota(jnp.int32, (8, nodes), 1)
    ancestor = lax.shift_right_logical(nodes + me, jnp.maximum(depths - 2 - row, 0))
    picks = ((lane == ancestor) & (row < depths - 2)).astype(BF)

    copies[0].wait()
    batch(rank, 16, lambda r: (transfer[r],), lambda e: dot(ident, e, NT), lambda r, v: put(wide_e, r * step, v))
    coeff[0:rank, :] = jnp.zeros((rank, coeff.shape[1]), BF)

    chip = lax.shift_right_logical(me, 1)
    half = rank // 2
    copies[1].wait()
    copies[2].wait()
    for held, core in ((mine, me & 1), (mate, 1 - (me & 1))):
        def place(q, got, core=core):
            seen = chip ^ q ^ (lax.shift_right_logical(q, 1) & 0b010101)
            coeff[pl.ds(pl.multiple_of((chips + seen) * rank + core * half, half), half), :] = got

        batch(chips, 16, lambda q, held=held: (held[rows_at(q, half), :],), lambda v: v, place)

    def e_of(node):
        return wide_e[0, pl.ds(node, rank, stride=step), :]

    def pair_work(left, right, kids):
        both = jnp.concatenate([left, right], axis=0).astype(BF)[:, 0:rank]
        return dot(both, kids, TN).astype(BF)

    count = chips // 2
    while count >= 4:
        def load(p, count=count):
            left = 2 * (count + p)
            return e_of(left), e_of(left + 1), coeff[rows_at(left, rank, 2), :]

        def store(p, got, count=count):
            coeff[rows_at(count + p, rank), :] = got

        batch(count, 32, load, pair_work, store)
        count //= 2

    copies[3].wait()
    batch(rank, 16, lambda r: (coupling[:, r].reshape(slots * rank, nodes),), lambda c: dot(picks, c, NT),
          lambda r, v: put(wide_c, r * 8, v))
    fars = []
    for depth in range(2, depths):
        node = lax.shift_right_logical(nodes + me, depths - depth)
        rhs = jnp.concatenate([coeff[rows_at(jnp.maximum(lists[s, node], 0), rank), :] for s in range(slots)], axis=0)
        lhs = jnp.concatenate(
            [wide_c[j, pl.ds(depth - 2, rank, stride=8), :].astype(BF) for j in range(wide_c.shape[0])], axis=1)
        fars.append((node, dot(lhs, rhs)))
    down = None
    for node, far in fars:
        down = far if down is None else far + dot(e_of(node).astype(BF)[:, 0:rank], down.astype(BF))
    out[...] = down.astype(BF)


def top(me, lists_t, mine, mate, transfer_t, coupling_t):
    rank, _, nodes = transfer_t.shape
    vecs = mine.shape[1]
    chunks = coupling_t.shape[0] * rank // 128
    sm = pl.BlockSpec(memory_space=pltpu.SMEM)
    hbm = pl.BlockSpec(memory_space=pltpu.HBM)
    return pl.pallas_call(
        top_kernel,
        in_specs=[sm, sm, ANY, ANY, hbm, hbm],
        out_shape=jax.ShapeDtypeStruct((rank, vecs), BF),
        scratch_shapes=[pltpu.VMEM(mine.shape, BF), pltpu.VMEM(mine.shape, BF), pltpu.VMEM(transfer_t.shape, BF), pltpu.VMEM(coupling_t.shape, BF),
                        pltpu.VMEM((1, rank * (nodes + PAD), 128), F32), pltpu.VMEM((chunks, rank * 8, 128), F32),
                        pltpu.VMEM((nodes * rank, vecs), BF), pltpu.SemaphoreType.DMA((4,))],
        compiler_params=pltpu.CompilerParams(vmem_limit_bytes=VMEM),
        cost_estimate=cost(4),
        name="top",
    )(me, lists_t, mine, mate, transfer_t, coupling_t)


def down_kernel(pos, blocks_in, transfer_in, own, mate, other, above, out, blocks, transfer, window, wide, down, sems):
    slots, rank, _, nodes = blocks.shape
    leaves = (nodes + 1) // 2
    rows = (nodes - FIRST) * rank
    part = rank // PARTS
    step = nodes + 1 + PAD
    width = (slots + 1) * rank
    chunks = wide.shape[0]
    ident = eye(nodes + 1, nodes)

    load_transfer = pltpu.make_async_copy(transfer_in, transfer, sems.at[0])
    load_blocks = [pltpu.make_async_copy(blocks_in.at[:, pl.ds(p * part, part)], blocks.at[:, pl.ds(p * part, part)],
                                         sems.at[1 + p]) for p in range(PARTS)]
    load_window = [pltpu.make_async_copy(src.at[pl.ds(FIRST * rank, rows)], window.at[pl.ds(n * rows, rows)],
                                         sems.at[1 + PARTS + n]) for n, src in enumerate((own, mate, other))]
    for c in [load_transfer] + load_blocks + load_window:
        c.start()
    window[3 * rows:3 * rows + rank, :] = jnp.zeros((rank, window.shape[1]), BF)
    load_transfer.wait()
    for p in range(PARTS):
        load_blocks[p].wait()
        batch(part, 8,
              lambda r, p=p: (jnp.concatenate(
                  [blocks[:, p * part + r].reshape(slots * rank, nodes), transfer[p * part + r]], axis=0),),
              lambda both: dot(ident, both, NT),
              lambda r, turned, p=p: put(wide, (p * part + r) * step, turned))

    def parent_of(node):
        if isinstance(node, int):
            return down[rows_at((node - 1) // 2, rank), :] if node else above[...]
        return down[rows_at(lax.shift_right_logical(node - 1, 1), rank), :]

    for node in range(FIRST):
        mine = wide[chunks - 1, pl.ds(node, rank, stride=step), :].astype(BF)[:, 0:rank]
        down[rows_at(node, rank), :] = dot(mine, parent_of(node)).astype(BF)
    for c in load_window:
        c.wait()

    def work(mine, rhs):
        lhs = jnp.concatenate([m.astype(BF) for m in mine], axis=1)[:, 0:width]
        return dot(lhs, rhs).astype(BF)

    count = FIRST + 1
    while count <= leaves:
        def load(p, count=count):
            node = count - 1 + p
            return ([wide[j, pl.ds(node, rank, stride=step), :] for j in range(chunks)],
                    jnp.concatenate([window[rows_at(pos[s, node], rank), :] for s in range(slots)]
                                    + [parent_of(node)], axis=0))

        def store(p, got, count=count):
            if count == leaves:
                out[rows_at(p, rank), :] = got
            else:
                down[rows_at(count - 1 + p, rank), :] = got

        batch(count, 64, load, work, store)
        count *= 2


PARTS = 4


def downward(pos, blocks_t, transfer_t, own, mate, other, above):
    slots, rank, _, nodes = blocks_t.shape
    leaves = (nodes + 1) // 2
    vecs = own.shape[1]
    rows = (nodes - FIRST) * rank
    chunks = ((slots + 1) * rank + 127) // 128
    hbm = pl.BlockSpec(memory_space=pltpu.HBM)
    return pl.pallas_call(
        down_kernel,
        in_specs=[pl.BlockSpec(memory_space=pltpu.SMEM)] + [hbm] * 2 + [ANY] * 3 + [pl.BlockSpec(memory_space=pltpu.VMEM)],
        out_shape=jax.ShapeDtypeStruct((leaves * rank, vecs), BF),
        scratch_shapes=[pltpu.VMEM(blocks_t.shape, BF), pltpu.VMEM(transfer_t.shape, BF),
                        pltpu.VMEM((3 * rows + rank, vecs), BF),
                        pltpu.VMEM((chunks, rank * (nodes + 1 + PAD), 128), F32),
                        pltpu.VMEM((leaves * rank, vecs), BF), pltpu.SemaphoreType.DMA((4 + PARTS,))],
        compiler_params=pltpu.CompilerParams(vmem_limit_bytes=40 << 20),
        cost_estimate=cost(11),
        name="downward",
    )(pos, blocks_t, transfer_t, own, mate, other, above)


def rows_kernel(parts, count, pos, down, *refs):
    lhs, pieces, (out, window, sems) = refs[:parts], refs[parts:parts + count], refs[parts + count:]
    i = pl.program_id(0)
    part, _, width = lhs[0].shape
    size = sum(a.shape[1] for a in lhs)
    rank = down.shape[0] // part
    slots = (width - rank) // size

    @pl.when(i == 0)
    def _():
        copies, at = [], 0
        for n, src in enumerate(pieces):
            copies.append(pltpu.make_async_copy(src, window.at[pl.ds(at, src.shape[0])], sems.at[n]))
            at += src.shape[0]
        for c in copies:
            c.start()
        window[at:at + size, :] = jnp.zeros((size, window.shape[1]), BF)
        for c in copies:
            c.wait()

    def load(l):
        return jnp.concatenate([a[l] for a in lhs], axis=0), jnp.concatenate(
            [window[rows_at(pos[s, i * part + l], size), :] for s in range(slots)] + [down[rows_at(l, rank), :]], axis=0)

    def store(l, got):
        out[rows_at(l, size), :] = got

    batch(part, 16, load, lambda a, b: dot(a, b).astype(BF), store)


def leaf_rows(pos, lhs, down, *pieces):
    leaves, _, width = lhs[0].shape
    size = sum(a.shape[1] for a in lhs)
    rows, vecs = pieces[0].shape
    rank = down.shape[0] // leaves
    part = 64
    any_ = pl.BlockSpec(memory_space=pl.ANY)
    return pl.pallas_call(
        lambda *refs: rows_kernel(len(lhs), len(pieces), *refs),
        grid_spec=pltpu.PrefetchScalarGridSpec(
            num_scalar_prefetch=1,
            grid=(leaves // part,),
            in_specs=[pl.BlockSpec((part * rank, vecs), lambda i, p: (i, 0))]
            + [pl.BlockSpec((part,) + a.shape[1:], lambda i, p: (i, 0, 0)) for a in lhs] + [any_] * len(pieces),
            out_specs=pl.BlockSpec((part * size, vecs), lambda i, p: (i, 0)),
            scratch_shapes=[pltpu.VMEM((3 * rows + size, vecs), BF), pltpu.SemaphoreType.DMA((len(pieces),))],
        ),
        out_shape=jax.ShapeDtypeStruct((rows, vecs), BF),
        compiler_params=pltpu.CompilerParams(vmem_limit_bytes=VMEM),
        cost_estimate=cost(6),
        name="leaf_rows",
    )(pos, down, *lhs, *pieces)


def head_kernel(src, dst, held, sems):
    rows = dst.shape[0]
    part = rows // 4
    at = [pl.ds(n * part, part) for n in range(4)]
    into = [pltpu.make_async_copy(src.at[a], held.at[a], sems.at[0, n]) for n, a in enumerate(at)]
    back = [pltpu.make_async_copy(held.at[a], dst.at[a], sems.at[1, n]) for n, a in enumerate(at)]
    for c in into:
        c.start()
    for c, d in zip(into, back):
        c.wait()
        d.start()
    for d in back:
        d.wait()


def head(value, rows):
    vecs = value.shape[1]
    hbm = pl.BlockSpec(memory_space=pltpu.HBM)
    return pl.pallas_call(
        head_kernel,
        in_specs=[hbm],
        out_specs=hbm,
        out_shape=jax.ShapeDtypeStruct((rows, vecs), BF),
        scratch_shapes=[pltpu.VMEM((rows, vecs), BF), pltpu.SemaphoreType.DMA((2, 4))],
        compiler_params=pltpu.CompilerParams(vmem_limit_bytes=MOST),
        cost_estimate=cost(2),
        name="head",
    )(value)


def slots_of(ids, level, own, base, per_slab):
    slab = lax.shift_right_arithmetic(ids, level)
    inside = ids & (lax.shift_left(jnp.ones_like(level), level) - 1)
    block = jnp.where(slab == own, 0, jnp.where(slab == (own ^ 1), 1, 2))
    return jnp.where(ids >= 0, block * per_slab + base + inside, 3 * per_slab)


def after(value, *marks):
    return lax.optimization_barrier((value,) + marks)[0]


def shards(points, leaf_basis, local_transfer, top_transfer, local_coupling, local_lists,
           top_coupling, top_lists, near_blocks, near_lists):
    leaf_dev, leaf_size, rank = leaf_basis.shape
    nodes = local_transfer.shape[0]
    count = lax.axis_size("leaf")
    own = lax.axis_index("leaf")
    mates = [(i, i ^ 1) for i in range(count)]
    others = [(i, i + 1) for i in range(1, count - 1, 2)]
    others = others + [(j, i) for i, j in others]

    def swap(value, pairs):
        return lax.ppermute(value, "leaf", pairs)

    def by_xor(value, bits):
        return swap(value, [(i, i ^ bits) for i in range(count)])

    basis_t = jnp.transpose(leaf_basis, (1, 2, 0))
    transfer_t = jnp.transpose(local_transfer, (1, 2, 0))
    near_t = jnp.transpose(near_blocks, (1, 2, 3, 0))
    coup_t = jnp.transpose(local_coupling, (1, 2, 3, 0))
    near_t = jnp.transpose(near_blocks, (1, 2, 3, 0))
    coup_t = jnp.transpose(local_coupling, (1, 2, 3, 0))
    cut = CUT * leaf_size
    early = head(points, cut)
    early_other = swap(early, others)
    coeff, keep, give, late = upward(own[None], after(points, early), basis_t, transfer_t, cut)
    gathered = (keep + swap(give, mates)).astype(BF)
    leaf_log = leaf_dev.bit_length() - 1
    near_pos = slots_of(near_lists.T, jnp.full((1, leaf_dev), leaf_log, jnp.int32), own, 0, leaf_dev)
    level = np.array([[(n + 1).bit_length() - 1 for n in range(nodes)]], np.int32)
    coup_pos = slots_of(local_lists.T, jnp.asarray(level), own, jnp.asarray(2 ** level - 1 - FIRST), nodes - FIRST)
    step = 2
    while step < count:
        came = [by_xor(gathered, way * step) for way in (1, 3, 2)]
        gathered = jnp.concatenate([gathered] + came, axis=0)
        if step == 2:
            gathered = after(gathered, early_other, near_pos, coup_pos)
        step *= 4
    gathered_mate = swap(gathered, mates)
    coeff_other = swap(after(coeff, came[0]), others)
    above = top(own[None], top_lists.T, gathered, gathered_mate, jnp.transpose(top_transfer, (1, 2, 0)),
                jnp.transpose(top_coupling, (1, 2, 3, 0)))
    late_other = swap(after(late, above), others)
    coeff_mate = swap(after(coeff, above), mates)
    points_mate = swap(after(points, above), mates)
    lhs_near = [turn(after(near_t, above), basis_t, "near_turn", 0, leaf_size)]
    above = after(above, lhs_near[0])
    down = downward(coup_pos, coup_t, transfer_t, coeff, coeff_mate, coeff_other, above)
    return leaf_rows(near_pos, lhs_near, down, points, points_mate, early_other, late_other)


CUT = 72


def solution(mesh):
    leaf, whole = P("leaf"), P()
    return jax.shard_map(
        shards,
        mesh=mesh,
        in_specs=(leaf, leaf, leaf, whole, leaf, leaf, whole, whole, leaf, leaf),
        out_specs=leaf,
        check_vma=False,
    )
```
